256 devices in a mesh: dp: 16 (over z, core), proto: 16 (over y, x).
Axes of the slice: x: 4, y: 4, z: 8, core: 2. Of those that a mesh axis runs over, the one named last changes fastest.
Arguments:
- teacher_emb: bfloat16 [8192, 256], P('dp'), may hold values from -0.8 to 0.8
- student_emb: bfloat16 [8192, 256], P('dp'), may hold values from -0.9 to 0.9
- prototypes: bfloat16 [65536, 256], P('proto'), may hold values from -0.36 to 0.36
Outputs:
- grad_student: float32 [8192, 256], P('dp')
- grad_protos: float32 [16, 4096, 256], P('proto', 'dp')
- mean_loss: float32 [], replicated
The draws below stay inside these ranges and needn't reach their ends.
All inputs are finite; a program needn't handle non-finite values.
Results may differ from the reference program's by a relative error of at most 0.006.
Values may be sent and summed in bfloat16 or wider, within the bound.
No kernel may reach another device: no remote copies, remote signals or barrier semaphores. Data moves between devices by JAX's collectives and lax.ppermute only.
A program may use at most 64 MiB of HBM per device.

```python
import jax
import jax.numpy as jnp
from jax import lax

D = 256
K = 65536
ITERS = 3
B = 8192
N_PROTO = 16


def proto_table(key):
    centers = jnp.clip(jax.random.normal(jax.random.fold_in(key, 12), (64, D), jnp.float32), -4.0, 4.0) / 16.0
    own_part = jnp.clip(jax.random.normal(jax.random.fold_in(key, 11), (K, D), jnp.float32), -4.0, 4.0) / 16.0
    spread_rows = jnp.repeat(centers, K // 64, axis=0)
    return 0.7071 * (spread_rows + own_part)


def crop_picks(key):
    member = K // 64
    first_draw = jax.random.randint(jax.random.fold_in(key, 26), (B,), 0, 64)
    second_draw = jax.random.randint(jax.random.fold_in(key, 27), (B,), 0, 64)
    third_draw = jax.random.randint(jax.random.fold_in(key, 28), (B,), 0, 64)
    cluster = jnp.minimum(jnp.minimum(first_draw, second_draw), third_draw)
    offset = jax.random.randint(jax.random.fold_in(key, 21), (B,), 0, member)
    return cluster * member + offset


def rough_noise(key, shape):
    return jnp.clip(jax.random.normal(key, shape, jnp.float32), -4.0, 4.0)


def draw_teacher_emb(key, part):
    table = proto_table(key)
    first_pick = crop_picks(key)
    key = jax.random.fold_in(key, 3)
    second_pick = jax.random.randint(jax.random.fold_in(key, 22), (B,), 0, K)
    noise_one = rough_noise(jax.random.fold_in(key, 23), (B, D))
    return (table[first_pick] + 0.6 * table[second_pick] + 0.7 * noise_one / 16.0).astype(jnp.bfloat16)


def draw_student_emb(key, part):
    table = proto_table(key)
    first_pick = crop_picks(key)
    key = jax.random.fold_in(key, 5)
    third_pick = jax.random.randint(jax.random.fold_in(key, 24), (B,), 0, K)
    noise_two = rough_noise(jax.random.fold_in(key, 25), (B, D))
    position = jnp.arange(B).astype(jnp.float32) / B
    weight_first = 1.5 - 1.2 * position
    return (weight_first[:, None] * table[first_pick] + 0.3 * table[third_pick] + 0.9 * noise_two / 16.0).astype(jnp.bfloat16)


def draw_prototypes(key, part):
    return proto_table(key).astype(jnp.bfloat16)


def setup_inputs(seed: int = 0) -> dict:
    keys = jax.random.split(jax.random.key(seed), 4)
    teacher_emb = draw_teacher_emb(jax.random.fold_in(keys[3], 71), 0)
    student_emb = draw_student_emb(jax.random.fold_in(keys[3], 71), 0)
    prototypes = draw_prototypes(jax.random.fold_in(keys[3], 71), 0)
    return dict(teacher_emb=teacher_emb, student_emb=student_emb, prototypes=prototypes)


def unit_rows(matrix):
    values = matrix.astype(jnp.float32)
    row_norms = jnp.sqrt(lax.optimization_barrier(jnp.sum(values * values, axis=-1, keepdims=True)) + 1e-06)
    return (values / row_norms, row_norms)

def reference(teacher_emb, student_emb, prototypes):
    t_unit, t_norms = unit_rows(teacher_emb)
    s_unit, s_norms = unit_rows(student_emb)
    w_unit, w_norms = unit_rows(prototypes)
    t_half = t_unit.astype(jnp.bfloat16)
    s_half = s_unit.astype(jnp.bfloat16)
    w_half = w_unit.astype(jnp.bfloat16)
    proto_blocks = w_half.reshape(N_PROTO, K // N_PROTO, D)

    def teacher_exp(proto_block):
        return jnp.exp(jnp.dot(t_half, proto_block.T, preferred_element_type=jnp.float32) / 0.07)

    def student_logits(proto_block):
        return jnp.dot(s_half, proto_block.T, preferred_element_type=jnp.float32) / 0.1
    row_scale = jnp.ones((B,), jnp.float32)
    col_blocks = jnp.ones((N_PROTO, K // N_PROTO), jnp.float32)
    for sweep_index in range(ITERS):

        def one_block(proto_block, row_scale=row_scale):
            expo_block = teacher_exp(proto_block)
            col_scale = 1.0 / lax.optimization_barrier(jnp.sum(expo_block * row_scale[:, None], axis=0))
            return (col_scale, lax.optimization_barrier(jnp.sum(expo_block * col_scale[None, :], axis=1)))
        col_blocks, row_parts = lax.map(one_block, proto_blocks)
        row_scale = 1.0 / lax.optimization_barrier(jnp.sum(row_parts, axis=0))
    totals = lax.optimization_barrier(jnp.sum(lax.map(lambda proto_block: lax.optimization_barrier(jnp.sum(jnp.exp(student_logits(proto_block)), axis=1)), proto_blocks), axis=0))
    lse_rows = jnp.log(totals)

    def final_block(running, inputs):
        proto_block, col_scale = inputs
        targets = teacher_exp(proto_block) * row_scale[:, None] * col_scale[None, :]
        logits = student_logits(proto_block)
        probs = jnp.exp(logits) / totals[:, None]
        loss_part = jnp.sum(targets * (logits - lse_rows[:, None]))
        grad_scores = ((probs - targets) / 0.1).astype(jnp.bfloat16)
        grad_s = jnp.dot(grad_scores, proto_block, preferred_element_type=jnp.float32)
        grad_w = jnp.dot(grad_scores.T, s_half, preferred_element_type=jnp.float32)
        return ((running[0] + loss_part, running[1] + grad_s), grad_w)
    start_carry = (jnp.zeros((), jnp.float32), jnp.zeros((B, D), jnp.float32))
    (loss_sum, grad_s), grad_w_blocks = lax.scan(final_block, start_carry, (proto_blocks, col_blocks))
    grad_student = (grad_s - s_unit * lax.optimization_barrier(jnp.sum(s_unit * grad_s, axis=-1, keepdims=True))) / s_norms
    grad_w = grad_w_blocks.reshape(K, D)
    grad_protos = (grad_w - w_unit * lax.optimization_barrier(jnp.sum(w_unit * grad_w, axis=-1, keepdims=True))) / w_norms
    mean_loss = -loss_sum / B
    return (grad_student, grad_protos.reshape(N_PROTO, K // N_PROTO, D), mean_loss)
```

```python
import jax
import jax.numpy as jnp
import numpy as np
from jax import lax
from jax.sharding import Mesh, PartitionSpec as P

ITERS = 3
CROPS = ("z", "core")
PROTOS = ("y", "x")


def unit_rows(matrix):
    values = matrix.astype(jnp.float32)
    row_norms = jnp.sqrt(jnp.sum(values * values, axis=-1, keepdims=True) + 1e-06)
    return (values / row_norms, row_norms)


def spread(part, axes, count):
    return lax.all_to_all(jnp.broadcast_to(part[None], (count,) + part.shape), axes, 0, 0)


def per_device(teacher_emb, student_emb, prototypes):
    crops = teacher_emb.shape[0]
    protos = prototypes.shape[0]
    n_dp = lax.axis_size("z") * lax.axis_size("core")
    n_proto = lax.axis_size("y") * lax.axis_size("x")

    def sum_dp(vec):
        return jnp.sum(spread(vec.reshape(-1, 128), CROPS, n_dp), axis=0).reshape(-1)

    def sum_proto(vec):
        return jnp.sum(spread(vec.reshape(-1, 128), PROTOS, n_proto), axis=0).reshape(-1)

    t_unit, t_norms = unit_rows(teacher_emb)
    s_unit, s_norms = unit_rows(student_emb)
    w_unit, w_norms = unit_rows(prototypes)
    t_half = t_unit.astype(jnp.bfloat16)
    s_half = s_unit.astype(jnp.bfloat16)
    w_half = w_unit.astype(jnp.bfloat16)
    contract_last = (((1,), (1,)), ((), ()))
    expo = jnp.exp(
        lax.dot_general(t_half, w_half, contract_last, preferred_element_type=jnp.float32) / 0.07
    )
    logits = (
        lax.dot_general(s_half, w_half, contract_last, preferred_element_type=jnp.float32) / 0.1
    )
    student_exp = jnp.exp(logits)
    col = 1.0 / sum_dp(jnp.sum(expo, axis=0))
    sums = sum_proto(
        jnp.concatenate([jnp.sum(expo * col[None, :], axis=1), jnp.sum(student_exp, axis=1)])
    )
    row, totals = 1.0 / sums[:crops], sums[crops:]
    col = 1.0 / sum_dp(jnp.sum(expo * row[:, None], axis=0))
    row = 1.0 / sum_proto(jnp.sum(expo * col[None, :], axis=1))
    col = 1.0 / sum_dp(jnp.sum(expo * row[:, None], axis=0))
    weighted = expo * col[None, :]
    sums = sum_proto(
        jnp.concatenate([jnp.sum(weighted, axis=1), jnp.sum(weighted * logits, axis=1)])
    )
    row = 1.0 / sums[:crops]
    loss_block = jnp.sum(row * sums[crops:] - jnp.log(totals))
    grad_scores = ((student_exp / totals[:, None] - weighted * row[:, None]) / 0.1).astype(
        jnp.bfloat16
    )
    contract_first = (((0,), (0,)), ((), ()))
    grad_w = lax.dot_general(
        grad_scores, s_half, contract_first, preferred_element_type=jnp.float32
    )
    owned = protos // n_dp
    grad_w = grad_w.astype(jnp.bfloat16).reshape(n_dp // 2, 2, owned, -1)
    core = lax.axis_index("core")
    keep = jnp.where(core == 0, grad_w[:, 0], grad_w[:, 1])
    give = jnp.where(core == 0, grad_w[:, 1], grad_w[:, 0])
    got = lax.ppermute(give, "core", [(0, 1), (1, 0)])
    half = (keep.astype(jnp.float32) + got.astype(jnp.float32)).astype(jnp.bfloat16)
    parts = lax.all_to_all(half, "z", 0, 0)
    proto_part = jnp.sum(parts.astype(jnp.float32), axis=0)

    grad_local = jnp.dot(grad_scores, w_half, preferred_element_type=jnp.float32)
    piece = lax.all_to_all(
        grad_local.astype(jnp.bfloat16).reshape(n_proto, crops // n_proto, -1), PROTOS, 0, 0
    )
    piece = jnp.sum(piece.astype(jnp.float32), axis=0)
    grad_s = spread(piece.astype(jnp.bfloat16), PROTOS, n_proto).reshape(crops, -1)
    grad_s = grad_s.astype(jnp.float32)
    loss_sum = jnp.sum(spread(jnp.broadcast_to(loss_block, (8, 128)), CROPS, n_dp)[:, 0, 0])
    mean_loss = -loss_sum / (crops * n_dp)
    grad_student = (grad_s - s_unit * jnp.sum(s_unit * grad_s, axis=-1, keepdims=True)) / s_norms
    first_owned = (lax.axis_index("z") * 2 + core) * owned
    w_mine = lax.dynamic_slice_in_dim(w_unit, first_owned, owned, 0)
    n_mine = lax.dynamic_slice_in_dim(w_norms, first_owned, owned, 0)
    grad_protos = (
        proto_part - w_mine * jnp.sum(w_mine * proto_part, axis=-1, keepdims=True)
    ) / n_mine
    return (grad_student, grad_protos[None], mean_loss)


def solution(mesh):
    fine = Mesh(np.asarray(mesh.devices).reshape(8, 2, 4, 4), ("z", "core", "y", "x"))
    in_specs = (P(CROPS, None), P(CROPS, None), P(PROTOS, None))
    out_specs = (P(CROPS, None), P(PROTOS, CROPS, None), P())
    return jax.shard_map(
        per_device, mesh=fine, in_specs=in_specs, out_specs=out_specs, check_vma=False
    )
```

```python
import functools

import jax
import jax.numpy as jnp
import numpy as np
from jax import lax
from jax.experimental import pallas as pl
from jax.experimental.pallas import tpu as pltpu
from jax.sharding import Mesh, PartitionSpec as P

CROPS = ("z", "core")
PROTOS = ("y", "x")
LOG2E = 1.4426950408889634
T_SCALE = LOG2E / 0.07
S_SCALE = LOG2E / 0.1
F32 = jnp.float32
BF16 = jnp.bfloat16
VMEM = pl.BlockSpec(memory_space=pltpu.VMEM)
SMEM = pl.BlockSpec(memory_space=pltpu.SMEM)
HBM = pl.BlockSpec(memory_space=pltpu.HBM)
LAST = (((1,), (1,)), ((), ()))
CHUNK = 512


def inverse_norms(values):
    return lax.rsqrt(jnp.sum(values * values, axis=-1, keepdims=True) + 1e-06)


def half_unit(block):
    values = block.astype(F32)
    return (values * inverse_norms(values)).astype(BF16)


def column(row):
    return jnp.broadcast_to(row, (128, 128)).T


def lay_down(block):
    return jnp.sum(block.T, axis=0, keepdims=True)


def twice(block):
    return jnp.concatenate([block, block], axis=1)


def call(kernel, out, operands, specs=None, outs=None, scratch=(), flops=0, limit=12):
    touched = sum(x.size * x.dtype.itemsize for x in operands)
    return pl.pallas_call(
        kernel,
        out_shape=out,
        in_specs=specs or [VMEM] * len(operands),
        out_specs=outs or jax.tree.map(lambda _: VMEM, out),
        scratch_shapes=list(scratch),
        cost_estimate=pl.CostEstimate(flops=flops, bytes_accessed=touched, transcendentals=0),
        compiler_params=pltpu.CompilerParams(vmem_limit_bytes=limit << 20),
    )(*operands)


def copies(pairs, sems):
    out = [pltpu.make_async_copy(a, b, sems.at[k]) for k, (a, b) in enumerate(pairs)]
    return out


def begin(pairs, sems):
    started = copies(pairs, sems)
    for c in started:
        c.start()
    return started


def lanes(k, size=CHUNK):
    return pl.ds(k * size, size)


def dp_place():
    return lax.axis_index("z") * lax.axis_size("core") + lax.axis_index("core")


def proto_place():
    return lax.axis_index("y") * lax.axis_size("x") + lax.axis_index("x")


def halves_kernel(t_hbm, s_hbm, th_ref, sh_ref, t_buf, s_buf, sems):
    one, two = begin([(t_hbm, t_buf), (s_hbm, s_buf)], sems)
    one.wait()
    th_ref[...] = half_unit(t_buf[...])
    two.wait()
    sh_ref[...] = half_unit(s_buf[...])


def teacher_kernel(n, th_ref, w_ref, e_ref, wh_ref, own_ref, msg_ref, sums):
    for j in range(w_ref.shape[0] // CHUNK):
        w_half = half_unit(w_ref[lanes(j), :])
        wh_ref[lanes(j), :] = w_half
        scores = lax.dot_general(th_ref[...], w_half, LAST, preferred_element_type=F32)
        expo = jnp.exp2(scores * T_SCALE)
        e_ref[:, lanes(j)] = expo.astype(BF16)
        part = jnp.sum(expo, axis=0, keepdims=True)
        for b in range(CHUNK // 128):
            at = j * (CHUNK // 128) + b
            sums[at : at + 1, :] = part[:, b * 128 : (b + 1) * 128]
    total = sums[...].astype(msg_ref.dtype)
    for k in range(n):
        msg_ref[k] = total
    owned = own_ref.shape[0]
    own_ref[...] = w_ref[pl.ds(pl.multiple_of(dp_place() * owned, owned), owned), :]


def student_kernel(sh_ref, wh_ref, tot_ref, p_ref, acc):
    for j in range(wh_ref.shape[0] // CHUNK):
        w_half = wh_ref[lanes(j), :]
        scores = lax.dot_general(sh_ref[...], w_half, LAST, preferred_element_type=F32)
        expo = jnp.exp2(scores * S_SCALE)
        part = sum(expo[:, b * 128 : (b + 1) * 128] for b in range(CHUNK // 128))
        prod = jnp.dot(expo.astype(BF16), w_half, preferred_element_type=F32)
        if j == 0:
            acc[...] = part
            p_ref[...] = prod
        else:
            acc[...] += part
            p_ref[...] += prod
    for i in range(4):
        tot_ref[i : i + 1, :] = lay_down(acc[lanes(i, 128), :])


def first_row_kernel(n, parts_ref, e_ref, tot_ref, p_ref, msg_ref, c_ref):
    size = CHUNK // n
    tails = [jnp.concatenate([row, tot_ref[i : i + 1, :]], axis=1)
             for i, row in enumerate(row_sums(parts_ref, e_ref, c_ref))]
    tail = jnp.concatenate(tails + [jnp.zeros((4, 256), F32)], axis=0)
    for k in range(n):
        msg_ref[k, 0:size, :] = p_ref[lanes(k, size), :]
        msg_ref[k, size : size + 8, :] = tail


def row_sums(parts_ref, e_ref, c_ref):
    c_ref[...] = 1.0 / jnp.sum(parts_ref[:, 0:32, :].astype(F32), axis=0)
    out = []
    for i in range(4):
        acc = jnp.zeros((128, 128), F32)
        for b in range(32):
            acc += e_ref[lanes(i, 128), b * 128 : (b + 1) * 128].astype(F32) * c_ref[b : b + 1, :]
        out.append(lay_down(acc))
    return out


def row_kernel(n, parts_ref, e_ref, msg_ref, c_ref):
    whole = jnp.concatenate(row_sums(parts_ref, e_ref, c_ref), axis=0)
    for k in range(n):
        msg_ref[k] = whole


def column_sums(scale, e_ref, row_col, out):
    for i in range(4):
        row_col[lanes(i, 128), :] = column(scale[i : i + 1])
    for b in range(32):
        acc = jnp.zeros((8, 128), F32)
        for i in range(4):
            rows = lanes(i, 128)
            prod = e_ref[rows, b * 128 : (b + 1) * 128].astype(F32) * row_col[rows, :]
            acc += jnp.sum(prod.reshape(16, 8, 128), axis=0)
        out[b : b + 1, :] = jnp.sum(acc, axis=0, keepdims=True)


def first_column_kernel(n, parts_ref, e_ref, msg_ref, tot_ref, p_ref, row_col, out):
    size = p_ref.shape[0]
    total = jnp.sum(parts_ref[...], axis=0)
    p_ref[...] = total[0:size]
    tot = total[size : size + 4, 128:256]
    tot_ref[...] = tot
    column_sums(1.0 / total[size : size + 4, 0:128], e_ref, row_col, out)
    whole = out[...].astype(BF16)
    high = tot.astype(BF16)
    low = (tot - high.astype(F32)).astype(BF16)
    tail = jnp.concatenate([high.astype(F32), low.astype(F32), jnp.zeros((8, 128), F32)], 0)
    tail = tail.astype(BF16)
    for k in range(n):
        msg_ref[k, 0:32, :] = whole
        msg_ref[k, 32:48, :] = tail


def column_kernel(n, parts_ref, e_ref, msg_ref, row_col, out):
    column_sums(1.0 / jnp.sum(parts_ref[...], axis=0), e_ref, row_col, out)
    whole = out[...]
    for k in range(n):
        msg_ref[k] = whole


def last_kernel(n, parts_ref, e_ref, wh_ref, sh_ref, msg_ref, c_ref, prod, acc):
    c_ref[...] = 1.0 / jnp.sum(parts_ref[...], axis=0)
    size = CHUNK // n
    for j in range(e_ref.shape[1] // CHUNK):
        pieces = []
        for b in range(CHUNK // 128):
            at = j * (CHUNK // 128) + b
            piece = e_ref[:, at * 128 : (at + 1) * 128].astype(F32) * c_ref[at : at + 1, :]
            pieces.append(piece)
        part = sum(pieces)
        scaled = jnp.concatenate([p.astype(BF16) for p in pieces], axis=1)
        term = jnp.dot(scaled, wh_ref[lanes(j), :], preferred_element_type=F32)
        if j == 0:
            acc[...] = part
            prod[...] = term
        else:
            acc[...] += part
            prod[...] += term
    tails = []
    for i in range(4):
        rows = lanes(i, 128)
        dots = prod[rows, :] * sh_ref[rows, :].astype(F32)
        dots = (dots[:, 0:128] + dots[:, 128:256]) * 10.0
        tails.append(jnp.concatenate([lay_down(acc[rows, :]), lay_down(dots)], axis=1))
    tail = jnp.concatenate(tails + [jnp.zeros((4, 256), F32)], axis=0)
    for k in range(n):
        msg_ref[k, 0:size, :] = prod[lanes(k, size), :]
        msg_ref[k, size : size + 8, :] = tail


def pick_rows(rows_ref, col_ref, me, size):
    per = 128 // size
    col_ref[...] = column(rows_ref[pl.ds(me // per, 1), :])
    return twice(col_ref[pl.ds(pl.multiple_of((me % per) * size, 8), size), :])


def crops_kernel(
    n_dp, n, parts_ref, tot_ref, p_ref, s_ref, rmsg_ref, gmsg_ref, rows_ref, col_ref
):
    size = CHUNK // n
    total = jnp.sum(parts_ref[...], axis=0)
    scale = 1.0 / total[size : size + 4, 0:128]
    tot = tot_ref[...]
    loss = jnp.sum(scale * total[size : size + 4, 128:256] - jnp.log(tot))
    whole = jnp.concatenate([scale, jnp.full((4, 128), loss, F32)], axis=0)
    for k in range(n_dp):
        rmsg_ref[k] = whole
    me = proto_place()
    rows_ref[...] = jnp.concatenate([scale, 1.0 / tot], axis=0)
    r_col = pick_rows(rows_ref.at[0:4], col_ref, me, size)
    tot_col = pick_rows(rows_ref.at[4:8], col_ref, me, size)
    grad = (p_ref[...] * tot_col - r_col * total[0:size]) * 10.0
    values = s_ref[pl.ds(pl.multiple_of(me * size, 16), size), :].astype(F32)
    inverse = inverse_norms(values)
    s_unit = values * inverse
    grad = (grad - s_unit * jnp.sum(s_unit * grad, axis=-1, keepdims=True)) * inverse
    grad = grad.astype(BF16)
    for k in range(n):
        gmsg_ref[k] = grad


def own_teacher_kernel(w_ref, t_ref, e_ref, done_ref):
    w_half = half_unit(w_ref[...])
    for d in range(t_ref.shape[0]):
        scores = lax.dot_general(w_half, t_ref[d], LAST, preferred_element_type=F32)
        e_ref[:, lanes(d)] = jnp.exp2(scores * T_SCALE).astype(BF16)
    done_ref[...] = jnp.zeros((8, 128), F32)


def own_student_kernel(w_ref, s_hbm, parts_ref, g_ref, s_buf, sems):
    blocks = s_buf.shape[0]
    fetched = begin([(s_hbm.at[d], s_buf.at[d]) for d in range(blocks)], sems)
    w_half = half_unit(w_ref[...])
    total = jnp.zeros((256, 256), F32)
    for d in range(blocks):
        fetched[d].wait()
        scores = lax.dot_general(w_half, s_buf[d], LAST, preferred_element_type=F32)
        tail = parts_ref[d, 32:48, :].astype(F32)
        inv = 1.0 / (tail[0:4] + tail[4:8])
        row = jnp.concatenate([inv[i : i + 1] for i in range(4)], axis=1)
        probs = (jnp.exp2(scores * S_SCALE) * row).astype(BF16)
        total += jnp.dot(probs, s_buf[d], preferred_element_type=F32)
    g_ref[...] = total


def protos_kernel(
    count, parts_ref, e_ref, s_ref, g_ref, c_ref, w_ref, piece_ref, out_ref, loss_ref, crop_ref
):
    size = piece_ref.shape[1]
    for k in range(piece_ref.shape[0]):
        crop_ref[lanes(k, size), :] = piece_ref[k].astype(F32)
    total = jnp.zeros((256, 256), F32)
    loss = jnp.zeros((1, 128), F32)
    for d in range(s_ref.shape[0]):
        row = jnp.concatenate([parts_ref[d, i : i + 1, :] for i in range(4)], axis=1)
        loss += parts_ref[d, 4:5, :]
        scaled = (e_ref[:, lanes(d)].astype(F32) * row).astype(BF16)
        total += jnp.dot(scaled, s_ref[d], preferred_element_type=F32)
    values = w_ref[...].astype(F32)
    inverse = inverse_norms(values)
    w_unit = values * inverse
    first = dp_place() * 2
    cols = [column(c_ref[pl.ds(first + k, 1), :]) for k in range(2)]
    cols = twice(jnp.concatenate(cols, axis=0))
    grad = (g_ref[...] - total * cols) * 10.0
    out_ref[...] = (grad - w_unit * jnp.sum(w_unit * grad, axis=-1, keepdims=True)) * inverse
    loss_ref[0, 0] = loss[0, 0] * (-1.0 / count)


def shape(dims, dtype=F32):
    return jax.ShapeDtypeStruct(dims, dtype)


def per_device(teacher_emb, student_emb, prototypes):
    n_dp = lax.axis_size("z") * lax.axis_size("core")
    n = lax.axis_size("y") * lax.axis_size("x")
    crops, width = teacher_emb.shape
    protos = prototypes.shape[0]
    owned = protos // n_dp
    size = crops // n
    to_dp = lambda msg: lax.all_to_all(msg, CROPS, 0, 0)
    to_proto = lambda msg: lax.all_to_all(msg, PROTOS, 0, 0)
    tie = lax.optimization_barrier
    vm = lambda dims, dtype=F32: pltpu.VMEM(dims, dtype)
    sems = lambda count: pltpu.SemaphoreType.DMA((count,))
    block_flops = 2 * crops * protos * width

    t_half, s_half = call(
        halves_kernel,
        (shape((crops, width), BF16), shape((crops, width), BF16)),
        (teacher_emb, student_emb),
        specs=[HBM, HBM],
        scratch=[vm((crops, width), BF16), vm((crops, width), BF16), sems(2)],
        limit=57,
    )
    t_all = lax.all_gather(t_half, CROPS)
    s_all = lax.all_gather(s_half, CROPS)

    expo, w_half, w_own, msg = call(
        functools.partial(teacher_kernel, n_dp),
        (
            shape((crops, protos), BF16), shape((protos, width), BF16),
            shape((owned, width), BF16), shape((n_dp, 32, 128), BF16),
        ),
        (t_half, prototypes),
        scratch=[vm((32, 128))],
        flops=block_flops,
    )
    tot_part, p_part = call(
        student_kernel,
        (shape((4, 128)), shape((crops, width))),
        (s_half, w_half),
        scratch=[vm((crops, 128))],
        flops=2 * block_flops,
    )
    msg, p_part = tie((msg, p_part))
    parts = to_dp(msg)
    msg = call(
        functools.partial(first_row_kernel, n),
        shape((n, size + 8, width)),
        (parts, expo, tot_part, p_part),
        scratch=[vm((32, 128))],
    )
    parts = to_proto(msg)
    column_scratch = [vm((crops, 128)), vm((32, 128))]
    msg, totals, p_sum = call(
        functools.partial(first_column_kernel, n_dp),
        (shape((n_dp, 48, 128), BF16), shape((4, 128)), shape((size, width))),
        (parts, expo),
        scratch=column_scratch,
    )
    tot_parts = to_dp(msg)
    msg = call(
        functools.partial(row_kernel, n),
        shape((n, 4, 128)),
        (tot_parts, expo),
        scratch=[vm((32, 128))],
    )
    msg, t_all = tie((msg, t_all))
    parts = to_proto(msg)
    parts, t_all = tie((parts, t_all))
    e_own, done = call(
        own_teacher_kernel,
        (shape((owned, n_dp * crops), BF16), shape((8, 128))),
        (w_own, t_all),
        flops=block_flops,
    )
    msg = call(
        functools.partial(column_kernel, n_dp),
        shape((n_dp, 32, 128)),
        (parts, expo),
        scratch=column_scratch,
    )
    msg, done = tie((msg, done))
    parts = to_dp(msg)
    msg, col = call(
        functools.partial(last_kernel, n),
        (shape((n, size + 8, width)), shape((32, 128))),
        (parts, expo, w_half, s_half),
        scratch=[vm((crops, width)), vm((crops, 128))],
        flops=block_flops,
    )
    parts = to_proto(msg)
    rmsg, gmsg = call(
        functools.partial(crops_kernel, n_dp, n),
        (shape((n_dp, 8, 128)), shape((n, size, width), BF16)),
        (parts, totals, p_sum, student_emb),
        scratch=[vm((8, 128)), vm((128, 128))],
    )
    s_all, rmsg = tie((s_all, rmsg))
    g_student = call(
        own_student_kernel,
        shape((owned, width)),
        (w_own, s_all, tot_parts),
        specs=[VMEM, HBM, VMEM],
        scratch=[vm((n_dp, crops, width), BF16), sems(n_dp)],
        flops=2 * block_flops,
        limit=57,
    )
    pieces = to_proto(gmsg)
    rmsg, g_student, pieces = tie((rmsg, g_student, pieces))
    parts = to_dp(rmsg)
    grad_protos, loss, grad_student = call(
        functools.partial(protos_kernel, float(crops * n_dp)),
        (shape((owned, width)), shape((1, 1)), shape((crops, width))),
        (parts, e_own, s_all, g_student, col, w_own, pieces),
        outs=(VMEM, SMEM, VMEM),
        flops=block_flops,
    )
    return grad_student, grad_protos[None], loss[0, 0]


def solution(mesh):
    fine = Mesh(np.asarray(mesh.devices).reshape(8, 2, 4, 4), ("z", "core", "y", "x"))
    in_specs = (P(CROPS, None), P(CROPS, None), P(PROTOS, None))
    out_specs = (P(CROPS, None), P(PROTOS, CROPS, None), P())
    return jax.shard_map(
        per_device, mesh=fine, in_specs=in_specs, out_specs=out_specs, check_vma=False
    )
```

```python
import functools

import jax
import jax.numpy as jnp
import numpy as np
from jax import lax
from jax.experimental import pallas as pl
from jax.experimental.pallas import tpu as pltpu
from jax.sharding import Mesh, PartitionSpec as P

CROPS = ("z", "core")
PROTOS = ("y", "x")
LOG2E = 1.4426950408889634
T_SCALE = LOG2E / 0.07
S_SCALE = LOG2E / 0.1
F32 = jnp.float32
BF16 = jnp.bfloat16
VMEM = pl.BlockSpec(memory_space=pltpu.VMEM)
SMEM = pl.BlockSpec(memory_space=pltpu.SMEM)
HBM = pl.BlockSpec(memory_space=pltpu.HBM)
LAST = (((1,), (1,)), ((), ()))
CHUNK = 512


def inverse_norms(values):
    return lax.rsqrt(jnp.sum(values * values, axis=-1, keepdims=True) + 1e-06)


def half_unit(block):
    values = block.astype(F32)
    return (values * inverse_norms(values)).astype(BF16)


def column(row):
    return jnp.broadcast_to(row, (128, 128)).T


def lay_down(block):
    return jnp.sum(block.T, axis=0, keepdims=True)


def twice(block):
    return jnp.concatenate([block, block], axis=1)


def call(kernel, out, operands, specs=None, outs=None, scratch=(), flops=0, limit=12):
    touched = sum(x.size * x.dtype.itemsize for x in operands)
    return pl.pallas_call(
        kernel,
        out_shape=out,
        in_specs=specs or [VMEM] * len(operands),
        out_specs=outs or jax.tree.map(lambda _: VMEM, out),
        scratch_shapes=list(scratch),
        cost_estimate=pl.CostEstimate(flops=flops, bytes_accessed=touched, transcendentals=0),
        compiler_params=pltpu.CompilerParams(vmem_limit_bytes=limit << 20),
    )(*operands)


def copies(pairs, sems):
    out = [pltpu.make_async_copy(a, b, sems.at[k]) for k, (a, b) in enumerate(pairs)]
    return out


def begin(pairs, sems):
    started = copies(pairs, sems)
    for c in started:
        c.start()
    return started


def lanes(k, size=CHUNK):
    return pl.ds(k * size, size)


def dp_place():
    return lax.axis_index("z") * lax.axis_size("core") + lax.axis_index("core")


def proto_place():
    return lax.axis_index("y") * lax.axis_size("x") + lax.axis_index("x")


def halves_kernel(t_hbm, s_hbm, th_ref, sh_ref, keep_t, keep_s, t_buf, s_buf, sems):
    one, two = begin([(t_hbm, t_buf), (s_hbm, s_buf)], sems)
    one.wait()
    half = half_unit(t_buf[...])
    th_ref[...] = half
    keep_t[...] = half
    two.wait()
    half = half_unit(s_buf[...])
    sh_ref[...] = half
    keep_s[...] = half


def teacher_kernel(n, th_ref, w_ref, e_ref, wh_ref, msg_ref, sums):
    for j in range(w_ref.shape[0] // CHUNK):
        w_half = half_unit(w_ref[lanes(j), :])
        wh_ref[lanes(j), :] = w_half
        scores = lax.dot_general(th_ref[...], w_half, LAST, preferred_element_type=F32)
        expo = jnp.exp2(scores * T_SCALE)
        e_ref[:, lanes(j)] = expo.astype(BF16)
        part = jnp.sum(expo, axis=0, keepdims=True)
        for b in range(CHUNK // 128):
            at = j * (CHUNK // 128) + b
            sums[at : at + 1, :] = part[:, b * 128 : (b + 1) * 128]
    total = sums[...].astype(msg_ref.dtype)
    for k in range(n):
        msg_ref[k] = total


def student_kernel(sh_ref, wh_ref, tot_ref, p_ref, acc):
    for j in range(wh_ref.shape[0] // CHUNK):
        w_half = wh_ref[lanes(j), :]
        scores = lax.dot_general(sh_ref[...], w_half, LAST, preferred_element_type=F32)
        expo = jnp.exp2(scores * S_SCALE)
        part = sum(expo[:, b * 128 : (b + 1) * 128] for b in range(CHUNK // 128))
        prod = jnp.dot(expo.astype(BF16), w_half, preferred_element_type=F32)
        if j == 0:
            acc[...] = part
            p_ref[...] = prod
        else:
            acc[...] += part
            p_ref[...] += prod
    for i in range(4):
        tot_ref[i : i + 1, :] = lay_down(acc[lanes(i, 128), :])


def first_row_kernel(n, parts_ref, e_ref, tot_ref, p_ref, msg_ref, c_ref):
    size = CHUNK // n
    tails = [jnp.concatenate([row, tot_ref[i : i + 1, :]], axis=1)
             for i, row in enumerate(row_sums(parts_ref, e_ref, c_ref))]
    tail = split_pair(jnp.concatenate(tails, axis=0))
    for k in range(n):
        msg_ref[k, 0:size, :] = p_ref[lanes(k, size), :].astype(BF16)
        msg_ref[k, size : size + 16, :] = tail


def split_pair(rows):
    high = rows.astype(BF16).astype(F32)
    zeros = jnp.zeros((8, rows.shape[1]), F32)
    return jnp.concatenate([high, rows - high, zeros], axis=0).astype(BF16)


def row_sums(parts_ref, e_ref, c_ref):
    c_ref[...] = 1.0 / jnp.sum(parts_ref[:, 0:32, :].astype(F32), axis=0)
    out = []
    for i in range(4):
        acc = jnp.zeros((128, 128), F32)
        for b in range(32):
            acc += e_ref[lanes(i, 128), b * 128 : (b + 1) * 128].astype(F32) * c_ref[b : b + 1, :]
        out.append(lay_down(acc))
    return out


def row_kernel(n, parts_ref, e_ref, msg_ref, c_ref):
    whole = jnp.concatenate(row_sums(parts_ref, e_ref, c_ref), axis=0)
    for k in range(n):
        msg_ref[k] = whole


def column_sums(scale, e_ref, row_col, out):
    for i in range(4):
        row_col[lanes(i, 128), :] = column(scale[i : i + 1])
    for b in range(32):
        acc = jnp.zeros((8, 128), F32)
        for i in range(4):
            rows = lanes(i, 128)
            prod = e_ref[rows, b * 128 : (b + 1) * 128].astype(F32) * row_col[rows, :]
            acc += jnp.sum(prod.reshape(16, 8, 128), axis=0)
        out[b : b + 1, :] = jnp.sum(acc, axis=0, keepdims=True)


def first_column_kernel(n, parts_ref, e_ref, msg_ref, tot_ref, p_ref, row_col, out):
    size = p_ref.shape[0]
    total = jnp.sum(parts_ref[...].astype(F32), axis=0)
    p_ref[...] = total[0:size]
    sums = total[size : size + 4] + total[size + 4 : size + 8]
    tot = sums[:, 128:256]
    tot_ref[...] = tot
    column_sums(1.0 / sums[:, 0:128], e_ref, row_col, out)
    whole = out[...].astype(BF16)
    tail = split_pair(tot)
    for k in range(n):
        msg_ref[k, 0:32, :] = whole
        msg_ref[k, 32:48, :] = tail


def column_kernel(parts_ref, e_ref, msg_ref, row_col):
    column_sums(1.0 / jnp.sum(parts_ref[...], axis=0), e_ref, row_col, msg_ref)


def last_kernel(n, parts_ref, e_ref, wh_ref, sh_ref, msg_ref, c_ref, prod, acc):
    c_ref[...] = 1.0 / jnp.sum(parts_ref[...], axis=0)
    size = CHUNK // n
    for j in range(e_ref.shape[1] // CHUNK):
        pieces = []
        for b in range(CHUNK // 128):
            at = j * (CHUNK // 128) + b
            piece = e_ref[:, at * 128 : (at + 1) * 128].astype(F32) * c_ref[at : at + 1, :]
            pieces.append(piece)
        part = sum(pieces)
        scaled = jnp.concatenate([p.astype(BF16) for p in pieces], axis=1)
        term = jnp.dot(scaled, wh_ref[lanes(j), :], preferred_element_type=F32)
        if j == 0:
            acc[...] = part
            prod[...] = term
        else:
            acc[...] += part
            prod[...] += term
    tails = []
    for i in range(4):
        rows = lanes(i, 128)
        dots = prod[rows, :] * sh_ref[rows, :].astype(F32)
        dots = (dots[:, 0:128] + dots[:, 128:256]) * 10.0
        tails.append(jnp.concatenate([lay_down(acc[rows, :]), lay_down(dots)], axis=1))
    tail = jnp.concatenate(tails + [jnp.zeros((4, 256), F32)], axis=0)
    for k in range(n):
        msg_ref[k, 0:size, :] = prod[lanes(k, size), :]
        msg_ref[k, size : size + 8, :] = tail


def pick_rows(rows_ref, col_ref, me, size):
    per = 128 // size
    col_ref[...] = column(rows_ref[pl.ds(me // per, 1), :])
    return twice(col_ref[pl.ds(pl.multiple_of((me % per) * size, 8), size), :])


def crops_kernel(
    n_dp, n, parts_ref, tot_ref, p_ref, s_ref, done_ref, rmsg_ref, gmsg_ref, rows_ref, col_ref
):
    size = CHUNK // n
    total = jnp.sum(parts_ref[...], axis=0)
    scale = 1.0 / total[size : size + 4, 0:128]
    tot = tot_ref[...]
    loss = jnp.sum(scale * total[size : size + 4, 128:256] - jnp.log(tot))
    whole = jnp.concatenate([scale, jnp.full((4, 128), loss, F32)], axis=0)
    for k in range(n_dp):
        rmsg_ref[k] = whole
    me = proto_place()
    rows_ref[...] = jnp.concatenate([scale, 1.0 / tot], axis=0)
    r_col = pick_rows(rows_ref.at[0:4], col_ref, me, size)
    tot_col = pick_rows(rows_ref.at[4:8], col_ref, me, size)
    grad = (p_ref[...] * tot_col - r_col * total[0:size]) * 10.0
    values = s_ref[pl.ds(pl.multiple_of(me * size, 16), size), :].astype(F32)
    inverse = inverse_norms(values)
    s_unit = values * inverse
    grad = (grad - s_unit * jnp.sum(s_unit * grad, axis=-1, keepdims=True)) * inverse
    grad = grad.astype(BF16)
    for k in range(n):
        gmsg_ref[k] = grad


def pairs_of(src, buf, step):
    return [(src.at[k : k + step], buf.at[k : k + step]) for k in range(0, buf.shape[0], step)]


def own_rows(w_hbm, w_buf):
    owned = w_buf.shape[0]
    return w_hbm.at[pl.ds(pl.multiple_of(dp_place() * owned, owned), owned), :]


def own_kernel(
    w_hbm, t_hbm, s_hbm, parts_ref, e_hbm, g_ref, done_ref,
    w_buf, t_buf, s_buf, e_buf, w_sem, t_sems, s_sems, e_sems,
):
    step = 4
    w_copies = begin([(own_rows(w_hbm, w_buf), w_buf)], w_sem)
    t_copies = begin(pairs_of(t_hbm, t_buf, step), t_sems)
    s_copies = begin(pairs_of(s_hbm, s_buf, step), s_sems)
    e_copies = copies(pairs_of(e_buf, e_hbm, step), e_sems)
    w_copies[0].wait()
    w_half = half_unit(w_buf[...])
    for k in range(len(t_copies)):
        t_copies[k].wait()
        for d in range(k * step, k * step + step):
            scores = lax.dot_general(w_half, t_buf[d], LAST, preferred_element_type=F32)
            e_buf[d] = jnp.exp2(scores * T_SCALE).astype(BF16)
        e_copies[k].start()
    total = jnp.zeros((256, 256), F32)
    for k in range(len(s_copies)):
        s_copies[k].wait()
        for d in range(k * step, k * step + step):
            scores = lax.dot_general(w_half, s_buf[d], LAST, preferred_element_type=F32)
            tail = parts_ref[d, 32:48, :].astype(F32)
            inv = 1.0 / (tail[0:4] + tail[4:8])
            row = jnp.concatenate([inv[i : i + 1] for i in range(4)], axis=1)
            probs = (jnp.exp2(scores * S_SCALE) * row).astype(BF16)
            total += jnp.dot(probs, s_buf[d], preferred_element_type=F32)
    g_ref[...] = total
    done_ref[...] = jnp.zeros((8, 128), F32)
    for c in e_copies:
        c.wait()


def protos_kernel(
    count, parts_ref, e_hbm, s_hbm, g_ref, c_ref, w_hbm, out_ref, loss_ref,
    w_buf, e_buf, s_buf, w_sem, e_sems, s_sems,
):
    step = 4
    w_copies = begin([(own_rows(w_hbm, w_buf), w_buf)], w_sem)
    e_copies = copies(pairs_of(e_hbm, e_buf, step), e_sems)
    s_copies = copies(pairs_of(s_hbm, s_buf, step), s_sems)
    for one, two in zip(e_copies, s_copies):
        one.start()
        two.start()
    w_copies[0].wait()
    values = w_buf[...].astype(F32)
    inverse = inverse_norms(values)
    w_unit = values * inverse
    first = dp_place() * 2
    cols = [column(c_ref[pl.ds(first + k, 1), :]) for k in range(2)]
    cols = twice(jnp.concatenate(cols, axis=0))
    total = jnp.zeros((256, 256), F32)
    loss = jnp.zeros((1, 128), F32)
    for k in range(len(e_copies)):
        e_copies[k].wait()
        s_copies[k].wait()
        for d in range(k * step, k * step + step):
            row = jnp.concatenate([parts_ref[d, i : i + 1, :] for i in range(4)], axis=1)
            loss += parts_ref[d, 4:5, :]
            scaled = (e_buf[d].astype(F32) * row).astype(BF16)
            total += jnp.dot(scaled, s_buf[d], preferred_element_type=F32)
    grad = (g_ref[...] - total * cols) * 10.0
    out_ref[...] = (grad - w_unit * jnp.sum(w_unit * grad, axis=-1, keepdims=True)) * inverse
    loss_ref[0, 0] = loss[0, 0] * (-1.0 / count)


def shape(dims, dtype=F32):
    return jax.ShapeDtypeStruct(dims, dtype)


def per_device(teacher_emb, student_emb, prototypes):
    n_dp = lax.axis_size("z") * lax.axis_size("core")
    n = lax.axis_size("y") * lax.axis_size("x")
    crops, width = teacher_emb.shape
    protos = prototypes.shape[0]
    owned = protos // n_dp
    size = crops // n
    to_dp = lambda msg: lax.all_to_all(msg, CROPS, 0, 0)
    to_proto = lambda msg: lax.all_to_all(msg, PROTOS, 0, 0)
    tie = lax.optimization_barrier
    vm = lambda dims, dtype=F32: pltpu.VMEM(dims, dtype)
    sems = lambda count: pltpu.SemaphoreType.DMA((count,))
    block_flops = 2 * crops * protos * width

    t_send, s_send, t_half, s_half = call(
        halves_kernel,
        (shape((crops, width), BF16),) * 4,
        (teacher_emb, student_emb),
        specs=[HBM, HBM],
        scratch=[vm((crops, width), BF16), vm((crops, width), BF16), sems(2)],
        limit=57,
    )
    t_all = lax.all_gather(t_send, CROPS)
    s_all = lax.all_gather(s_send, CROPS)

    expo, w_half, msg = call(
        functools.partial(teacher_kernel, n_dp),
        (
            shape((crops, protos), BF16), shape((protos, width), BF16),
            shape((n_dp, 32, 128), BF16),
        ),
        (t_half, prototypes),
        scratch=[vm((32, 128))],
        flops=block_flops,
    )
    tot_part, p_part = call(
        student_kernel,
        (shape((4, 128)), shape((crops, width))),
        (s_half, w_half),
        scratch=[vm((crops, 128))],
        flops=2 * block_flops,
    )
    msg, p_part = tie((msg, p_part))
    parts = to_dp(msg)
    msg = call(
        functools.partial(first_row_kernel, n),
        shape((n, size + 16, width), BF16),
        (parts, expo, tot_part, p_part),
        scratch=[vm((32, 128))],
    )
    parts = to_proto(msg)
    column_scratch = [vm((crops, 128)), vm((32, 128))]
    msg, totals, p_sum = call(
        functools.partial(first_column_kernel, n_dp),
        (shape((n_dp, 48, 128), BF16), shape((4, 128)), shape((size, width))),
        (parts, expo),
        scratch=column_scratch,
    )
    tot_parts = to_dp(msg)
    msg = call(
        functools.partial(row_kernel, n),
        shape((n, 4, 128)),
        (tot_parts, expo),
        scratch=[vm((32, 128))],
    )
    parts = to_proto(msg)
    msg = call(
        column_kernel,
        shape((32, 128)),
        (parts, expo),
        scratch=column_scratch[:1],
    )
    msg = msg + lax.ppermute(msg, "core", [(0, 1), (1, 0)])
    parts = lax.all_to_all(jnp.broadcast_to(msg, (lax.axis_size("z"), 32, 128)), "z", 0, 0)
    msg, col = call(
        functools.partial(last_kernel, n),
        (shape((n, size + 8, width)), shape((32, 128))),
        (parts, expo, w_half, s_half),
        scratch=[vm((crops, width)), vm((crops, 128))],
        flops=block_flops,
    )
    msg, t_all = tie((msg, t_all))
    blocks = lambda rows, columns: vm((n_dp, rows, columns), BF16)
    e_own, g_student, done = call(
        own_kernel,
        (shape((n_dp, owned, crops), BF16), shape((owned, width)), shape((8, 128))),
        (prototypes, t_all, s_all, tot_parts),
        specs=[HBM, HBM, HBM, VMEM],
        outs=(HBM, VMEM, VMEM),
        scratch=[
            vm((owned, width), BF16),
            blocks(crops, width), blocks(crops, width), blocks(owned, crops),
            sems(1), sems(4), sems(4), sems(4),
        ],
        flops=3 * block_flops,
        limit=57,
    )
    parts = to_proto(msg)
    rmsg, gmsg = call(
        functools.partial(crops_kernel, n_dp, n),
        (shape((n_dp, 8, 128)), shape((n, size, width), BF16)),
        (parts, totals, p_sum, student_emb, done),
        scratch=[vm((8, 128)), vm((128, 128))],
    )
    parts = to_dp(rmsg)
    parts, gmsg = tie((parts, gmsg))
    pieces = to_proto(gmsg)
    grad_protos, loss = call(
        functools.partial(protos_kernel, float(crops * n_dp)),
        (shape((owned, width)), shape((1, 1))),
        (parts, e_own, s_all, g_student, col, prototypes),
        specs=[VMEM, HBM, HBM, VMEM, VMEM, HBM],
        outs=(VMEM, SMEM),
        scratch=[
            vm((owned, width), BF16), blocks(owned, crops), blocks(crops, width),
            sems(1), sems(4), sems(4),
        ],
        flops=block_flops,
        limit=57,
    )
    grad_student = pieces.astype(F32).reshape(crops, width)
    return grad_student, grad_protos[None], loss[0, 0]


def solution(mesh):
    fine = Mesh(np.asarray(mesh.devices).reshape(8, 2, 4, 4), ("z", "core", "y", "x"))
    in_specs = (P(CROPS, None), P(CROPS, None), P(PROTOS, None))
    out_specs = (P(CROPS, None), P(PROTOS, CROPS, None), P())
    return jax.shard_map(
        per_device, mesh=fine, in_specs=in_specs, out_specs=out_specs, check_vma=False
    )
```

```python
import functools

import jax
import jax.numpy as jnp
import numpy as np
from jax import lax
from jax.experimental import pallas as pl
from jax.experimental.pallas import tpu as pltpu
from jax.sharding import Mesh, PartitionSpec as P

CROPS = ("z", "core")
PROTOS = ("y", "x")
LOG2E = 1.4426950408889634
T_SCALE = LOG2E / 0.07
S_SCALE = LOG2E / 0.1
F32 = jnp.float32
BF16 = jnp.bfloat16
VMEM = pl.BlockSpec(memory_space=pltpu.VMEM)
SMEM = pl.BlockSpec(memory_space=pltpu.SMEM)
HBM = pl.BlockSpec(memory_space=pltpu.HBM)
LAST = (((1,), (1,)), ((), ()))
CHUNK = 512


def inverse_norms(values):
    return lax.rsqrt(jnp.sum(values * values, axis=-1, keepdims=True) + 1e-06)


def half_unit(block):
    values = block.astype(F32)
    return (values * inverse_norms(values)).astype(BF16)


def column(row):
    return jnp.broadcast_to(row, (128, 128)).T


def lay_down(block):
    return jnp.sum(block.T, axis=0, keepdims=True)


def twice(block):
    return jnp.concatenate([block, block], axis=1)


def call(kernel, out, operands, specs=None, outs=None, scratch=(), flops=0, limit=12):
    touched = sum(x.size * x.dtype.itemsize for x in operands)
    return pl.pallas_call(
        kernel,
        out_shape=out,
        in_specs=specs or [VMEM] * len(operands),
        out_specs=outs or jax.tree.map(lambda _: VMEM, out),
        scratch_shapes=list(scratch),
        cost_estimate=pl.CostEstimate(flops=flops, bytes_accessed=touched, transcendentals=0),
        compiler_params=pltpu.CompilerParams(vmem_limit_bytes=limit << 20),
    )(*operands)


def copies(pairs, sems):
    out = [pltpu.make_async_copy(a, b, sems.at[k]) for k, (a, b) in enumerate(pairs)]
    return out


def begin(pairs, sems):
    started = copies(pairs, sems)
    for c in started:
        c.start()
    return started


def lanes(k, size=CHUNK):
    return pl.ds(k * size, size)


def dp_place():
    return lax.axis_index("z") * lax.axis_size("core") + lax.axis_index("core")


def proto_place():
    return lax.axis_index("y") * lax.axis_size("x") + lax.axis_index("x")


def teacher_kernel(n, t_ref, s_ref, w_ref, x_ref, sh_ref, e0, e1, wh_ref, msg_ref, sums):
    t_half = half_unit(t_ref[...])
    x_ref[0] = t_half
    for j in range(w_ref.shape[0] // CHUNK):
        w_half = half_unit(w_ref[lanes(j), :])
        wh_ref[lanes(j), :] = w_half
        scores = lax.dot_general(x_ref[0], w_half, LAST, preferred_element_type=F32)
        expo = jnp.exp2(scores * T_SCALE)
        for i, e_ref in enumerate((e0, e1)):
            e_ref[:, lanes(j)] = expo[i * 256 : (i + 1) * 256].astype(BF16)
        part = jnp.sum(expo, axis=0, keepdims=True)
        for b in range(CHUNK // 128):
            at = j * (CHUNK // 128) + b
            sums[at : at + 1, :] = part[:, b * 128 : (b + 1) * 128]
    total = sums[...].astype(msg_ref.dtype)
    for k in range(n):
        msg_ref[k] = total
    s_half = half_unit(s_ref[...])
    x_ref[1] = s_half
    sh_ref[...] = s_half


def student_kernel(sh_ref, wh_ref, tot_ref, p_ref, acc):
    for j in range(wh_ref.shape[0] // CHUNK):
        w_half = wh_ref[lanes(j), :]
        scores = lax.dot_general(sh_ref[...], w_half, LAST, preferred_element_type=F32)
        expo = jnp.exp2(scores * S_SCALE)
        part = sum(expo[:, b * 128 : (b + 1) * 128] for b in range(CHUNK // 128))
        prod = jnp.dot(expo.astype(BF16), w_half, preferred_element_type=F32)
        if j == 0:
            acc[...] = part
            p_ref[...] = prod
        else:
            acc[...] += part
            p_ref[...] += prod
    for i in range(4):
        tot_ref[i : i + 1, :] = lay_down(acc[lanes(i, 128), :])


def first_row_kernel(n, parts_ref, e0, e1, tot_ref, p_ref, msg_ref, c_ref):
    size = CHUNK // n
    tails = [jnp.concatenate([row, tot_ref[i : i + 1, :]], axis=1)
             for i, row in enumerate(row_sums(parts_ref, (e0, e1), c_ref))]
    tail = split_pair(jnp.concatenate(tails, axis=0))
    for k in range(n):
        msg_ref[k, 0:size, :] = p_ref[lanes(k, size), :].astype(BF16)
        msg_ref[k, size : size + 16, :] = tail


def split_pair(rows):
    high = rows.astype(BF16).astype(F32)
    zeros = jnp.zeros((8, rows.shape[1]), F32)
    return jnp.concatenate([high, rows - high, zeros], axis=0).astype(BF16)


def row_sums(parts_ref, e_refs, c_ref):
    c_ref[...] = 1.0 / jnp.sum(parts_ref[:, 0:32, :].astype(F32), axis=0)
    out = []
    for i in range(4):
        rows = lanes(i % 2, 128)
        acc = jnp.zeros((128, 128), F32)
        for b in range(32):
            part = e_refs[i // 2][rows, b * 128 : (b + 1) * 128].astype(F32)
            acc += part * c_ref[b : b + 1, :]
        out.append(lay_down(acc))
    return out


def row_kernel(n, parts_ref, e0, e1, msg_ref, c_ref):
    whole = jnp.concatenate(row_sums(parts_ref, (e0, e1), c_ref), axis=0)
    for k in range(n):
        msg_ref[k] = whole


def column_sums(scale, e_refs, row_col, out):
    for i in range(4):
        row_col[lanes(i, 128), :] = column(scale[i : i + 1])
    for b in range(32):
        acc = jnp.zeros((8, 128), F32)
        for i in range(4):
            rows = lanes(i, 128)
            part = e_refs[i // 2][lanes(i % 2, 128), b * 128 : (b + 1) * 128].astype(F32)
            prod = part * row_col[rows, :]
            acc += jnp.sum(prod.reshape(16, 8, 128), axis=0)
        out[b : b + 1, :] = jnp.sum(acc, axis=0, keepdims=True)


def first_column_kernel(n, parts_ref, e0, e1, msg_ref, tot_ref, p_ref, row_col, out):
    size = p_ref.shape[0]
    total = jnp.sum(parts_ref[...].astype(F32), axis=0)
    p_ref[...] = total[0:size]
    sums = total[size : size + 4] + total[size + 4 : size + 8]
    tot = sums[:, 128:256]
    tot_ref[...] = tot
    column_sums(1.0 / sums[:, 0:128], (e0, e1), row_col, out)
    whole = out[...].astype(BF16)
    tail = split_pair(tot)
    for k in range(n):
        msg_ref[k, 0:32, :] = whole
        msg_ref[k, 32:48, :] = tail


def column_kernel(parts_ref, e0, e1, msg_ref, row_col):
    column_sums(1.0 / jnp.sum(parts_ref[...], axis=0), (e0, e1), row_col, msg_ref)


def last_kernel(n, parts_ref, e0, e1, wh_ref, sh_ref, msg_ref, c_ref, prod, acc):
    c_ref[...] = 1.0 / jnp.sum(parts_ref[...], axis=0)
    size = CHUNK // n
    for j in range(e0.shape[1] // CHUNK):
        pieces = []
        for b in range(CHUNK // 128):
            at = j * (CHUNK // 128) + b
            span = slice(at * 128, (at + 1) * 128)
            piece = jnp.concatenate([e[:, span] for e in (e0, e1)], axis=0)
            pieces.append(piece.astype(F32) * c_ref[at : at + 1, :])
        part = sum(pieces)
        scaled = jnp.concatenate([p.astype(BF16) for p in pieces], axis=1)
        term = jnp.dot(scaled, wh_ref[lanes(j), :], preferred_element_type=F32)
        if j == 0:
            acc[...] = part
            prod[...] = term
        else:
            acc[...] += part
            prod[...] += term
    tails = []
    for i in range(4):
        rows = lanes(i, 128)
        dots = prod[rows, :] * sh_ref[rows, :].astype(F32)
        dots = (dots[:, 0:128] + dots[:, 128:256]) * 10.0
        tails.append(jnp.concatenate([lay_down(acc[rows, :]), lay_down(dots)], axis=1))
    tail = jnp.concatenate(tails + [jnp.zeros((4, 256), F32)], axis=0)
    for k in range(n):
        msg_ref[k, 0:size, :] = prod[lanes(k, size), :]
        msg_ref[k, size : size + 8, :] = tail


def pick_rows(rows_ref, col_ref, me, size):
    per = 128 // size
    col_ref[...] = column(rows_ref[pl.ds(me // per, 1), :])
    return twice(col_ref[pl.ds(pl.multiple_of((me % per) * size, 8), size), :])


def crops_kernel(
    n_z, n, parts_ref, tot_ref, p_ref, s_ref, rmsg_ref, gmsg_ref, rows_ref, col_ref
):
    size = CHUNK // n
    total = jnp.sum(parts_ref[...], axis=0)
    scale = 1.0 / total[size : size + 4, 0:128]
    tot = tot_ref[...]
    loss = jnp.sum(scale * total[size : size + 4, 128:256] - jnp.log(tot))
    whole = jnp.concatenate([scale, jnp.full((4, 128), loss, F32)], axis=0)
    for k in range(n_z):
        rmsg_ref[k] = whole
    me = proto_place()
    rows_ref[...] = jnp.concatenate([scale, 1.0 / tot], axis=0)
    r_col = pick_rows(rows_ref.at[0:4], col_ref, me, size)
    tot_col = pick_rows(rows_ref.at[4:8], col_ref, me, size)
    grad = (p_ref[...] * tot_col - r_col * total[0:size]) * 10.0
    values = s_ref[pl.ds(pl.multiple_of(me * size, 16), size), :].astype(F32)
    inverse = inverse_norms(values)
    s_unit = values * inverse
    grad = (grad - s_unit * jnp.sum(s_unit * grad, axis=-1, keepdims=True)) * inverse
    grad = grad.astype(BF16)
    for k in range(n):
        gmsg_ref[k] = grad


HOPS = (0, -1, 1, -2, 2, -3, 3, -4)


def slot_place(k):
    n_z = lax.axis_size("z")
    return lax.rem(lax.axis_index("z") + HOPS[k] + n_z, n_z)


def chip_rows(w_hbm, w_buf):
    rows = w_buf.shape[0]
    return w_hbm.at[pl.ds(pl.multiple_of(lax.axis_index("z") * rows, rows), rows), :]


def student_term(w_half, s_half, parts_ref, k):
    scores = lax.dot_general(w_half, s_half, LAST, preferred_element_type=F32)
    tail = parts_ref[slot_place(k) * 2 + lax.axis_index("core"), 32:48, :].astype(F32)
    inv = 1.0 / (tail[0:4] + tail[4:8])
    row = jnp.concatenate([inv[i : i + 1] for i in range(4)], axis=1)
    probs = (jnp.exp2(scores * S_SCALE) * row).astype(BF16)
    return jnp.dot(probs, s_half, preferred_element_type=F32)


def own_teacher_kernel(w_hbm, *refs):
    blocks = refs[:8]
    parts_ref, e_hbm, g_ref, w_buf, t_buf, s_buf, e_buf, w_sem, t_sems, s_sem, e_sems = refs[8:]
    w_copies = begin([(chip_rows(w_hbm, w_buf), w_buf)], w_sem)
    t_copies = begin([(x.at[0], t_buf.at[k]) for k, x in enumerate(blocks)], t_sems)
    s_copies = begin([(blocks[7].at[1], s_buf)], s_sem)
    e_copies = copies([(e_buf.at[k], e_hbm.at[k]) for k in range(8)], e_sems)
    w_copies[0].wait()
    w_half = half_unit(w_buf[...])
    for k in range(8):
        t_copies[k].wait()
        scores = lax.dot_general(w_half, t_buf[k], LAST, preferred_element_type=F32)
        e_buf[k] = jnp.exp2(scores * T_SCALE).astype(BF16)
        e_copies[k].start()
    s_copies[0].wait()
    g_ref[...] = student_term(w_half, s_buf[...], parts_ref, 7)
    for c in e_copies:
        c.wait()


def own_student_kernel(w_hbm, *refs):
    blocks = refs[:7]
    parts_ref, g_ref, w_buf, s_buf, total, w_sem, s_sems = refs[7:]
    w_copies = begin([(chip_rows(w_hbm, w_buf), w_buf)], w_sem)
    s_copies = begin([(x.at[1], s_buf.at[k]) for k, x in enumerate(blocks)], s_sems)
    w_copies[0].wait()
    w_half = half_unit(w_buf[...])
    for k in range(7):
        s_copies[k].wait()
        term = student_term(w_half, s_buf[k], parts_ref, k)
        if k == 0:
            total[...] = term
        else:
            total[...] += term
    g_ref[...] = total[...]


def protos_kernel(parts_ref, e_hbm, g_ref, late_ref, c_ref, w_hbm, *refs):
    blocks = refs[:8]
    keep_ref, give_ref, own_ref, e_buf, s_buf, total, w_sem, e_sems, s_sems = refs[8:]
    half = own_ref.shape[0]
    start = pl.multiple_of(dp_place() * half, half)
    w_copies = begin([(w_hbm.at[pl.ds(start, half), :], own_ref)], w_sem)
    e_copies = copies([(e_hbm.at[k], e_buf.at[k]) for k in range(8)], e_sems)
    s_copies = copies([(x.at[1], s_buf.at[k]) for k, x in enumerate(blocks)], s_sems)
    for one, two in zip(e_copies, s_copies):
        one.start()
        two.start()
    first = lax.axis_index("z") * 4
    cols = [column(c_ref[pl.ds(first + i, 1), :]) for i in range(4)]
    loss = jnp.zeros((1, 128), F32)
    for k in range(8):
        z = slot_place(k)
        row = jnp.concatenate([parts_ref[z, i : i + 1, :] for i in range(4)], axis=1)
        loss += parts_ref[z, 4:5, :]
        e_copies[k].wait()
        scaled = (e_buf[k].astype(F32) * row).astype(BF16)
        s_copies[k].wait()
        term = jnp.dot(scaled, s_buf[k], preferred_element_type=F32)
        if k == 0:
            total[...] = term
        else:
            total[...] += term
    for i in range(4):
        rows = lanes(i, 128)
        total[rows, :] = (
            g_ref[rows, :] + late_ref[rows, :] - total[rows, :] * twice(cols[i])
        ) * 10.0
    core = lax.axis_index("core")
    keep_ref[0:half, :] = total[pl.ds(pl.multiple_of(core * half, half), half), :]
    give_ref[0:half, :] = total[pl.ds(pl.multiple_of((1 - core) * half, half), half), :]
    loss = twice(jnp.broadcast_to(loss, (8, 128)))
    give_ref[half : half + 8, :] = loss
    keep_ref[half : half + 8, :] = loss
    w_copies[0].wait()
    keep_ref[half + 8 : 2 * half + 8, :] = own_ref[...].astype(F32)


def finish_kernel(count, keep_ref, got_ref, out_ref, mean_ref):
    half = out_ref.shape[0]
    values = keep_ref[half + 8 : 2 * half + 8, :]
    inverse = inverse_norms(values)
    w_unit = values * inverse
    grad = keep_ref[0:half, :] + got_ref[0:half, :]
    loss = keep_ref[half : half + 1, :] + got_ref[half : half + 1, :]
    out_ref[...] = (grad - w_unit * jnp.sum(w_unit * grad, axis=-1, keepdims=True)) * inverse
    mean_ref[0, 0] = loss[0, 0] * (-1.0 / count)


def shape(dims, dtype=F32):
    return jax.ShapeDtypeStruct(dims, dtype)


def per_device(teacher_emb, student_emb, prototypes):
    n_z = lax.axis_size("z")
    n_dp = n_z * lax.axis_size("core")
    n = lax.axis_size("y") * lax.axis_size("x")
    crops, width = teacher_emb.shape
    protos = prototypes.shape[0]
    owned = protos // n_dp
    size = crops // n
    to_dp = lambda msg: lax.all_to_all(msg, CROPS, 0, 0)
    to_proto = lambda msg: lax.all_to_all(msg, PROTOS, 0, 0)
    tie = lax.optimization_barrier
    vm = lambda dims, dtype=F32: pltpu.VMEM(dims, dtype)
    sems = lambda count: pltpu.SemaphoreType.DMA((count,))
    block_flops = 2 * crops * protos * width

    right = lambda x: lax.ppermute(x, "z", [(i, (i + 1) % n_z) for i in range(n_z)])
    left = lambda x: lax.ppermute(x, "z", [(i, (i - 1) % n_z) for i in range(n_z)])
    swap = lambda x: lax.ppermute(x, "core", [(0, 1), (1, 0)])

    here, s_half, *expo, w_half, msg = call(
        functools.partial(teacher_kernel, n_dp),
        (
            shape((2, crops, width), BF16), shape((crops, width), BF16),
            *[shape((crops // 2, protos), BF16)] * 2, shape((protos, width), BF16),
            shape((n_dp, 32, 128), BF16),
        ),
        (teacher_emb, student_emb, prototypes),
        scratch=[vm((32, 128))],
        flops=block_flops,
    )
    a1, b1 = right(here), left(here)
    tot_part, p_part = call(
        student_kernel,
        (shape((4, 128)), shape((crops, width))),
        (s_half, w_half),
        scratch=[vm((crops, 128))],
        flops=2 * block_flops,
    )
    msg, p_part = tie((msg, p_part))
    parts = to_dp(msg)
    parts, a1, b1 = tie((parts, a1, b1))
    a2, b2 = right(a1), left(b1)
    msg = call(
        functools.partial(first_row_kernel, n),
        shape((n, size + 16, width), BF16),
        (parts, *expo, tot_part, p_part),
        scratch=[vm((32, 128))],
    )
    parts = to_proto(msg)
    column_scratch = [vm((crops, 128)), vm((32, 128))]
    msg, totals, p_sum = call(
        functools.partial(first_column_kernel, n_dp),
        (shape((n_dp, 48, 128), BF16), shape((4, 128)), shape((size, width))),
        (parts, *expo),
        scratch=column_scratch,
    )
    tot_parts = to_dp(msg)
    msg = call(
        functools.partial(row_kernel, n),
        shape((n, 4, 128)),
        (tot_parts, *expo),
        scratch=[vm((32, 128))],
    )
    msg, a2, b2 = tie((msg, a2, b2))
    a3, b3 = right(a2), left(b2)
    parts = to_proto(msg)
    msg = call(
        column_kernel,
        shape((32, 128)),
        (parts, *expo),
        scratch=column_scratch[:1],
    )
    msg = msg + swap(msg)
    to_z = lambda msg: lax.all_to_all(msg, "z", 0, 0)
    parts = to_z(jnp.broadcast_to(msg, (n_z, 32, 128)))
    parts, a3, b3 = tie((parts, a3, b3))
    a4 = right(a3)
    gathered = (here, a1, b1, a2, b2, a3, b3, a4)
    msg, col = call(
        functools.partial(last_kernel, n),
        (shape((n, size + 8, width)), shape((32, 128))),
        (parts, *expo, w_half, s_half),
        scratch=[vm((crops, width)), vm((crops, 128))],
        flops=block_flops,
    )
    msg, *gathered = tie((msg,) + gathered[:-1])
    gathered = tuple(gathered) + (a4,)
    blocks = lambda rows, columns: vm((n_z, rows, columns), BF16)
    chip = 2 * owned
    g_student = call(
        own_student_kernel,
        shape((chip, width)),
        (prototypes,) + gathered[:-1] + (tot_parts,),
        specs=[HBM] * 8 + [VMEM],
        scratch=[
            vm((chip, width), BF16), blocks(crops, width), vm((chip, width)), sems(1), sems(n_z),
        ],
        flops=2 * block_flops,
        limit=57,
    )
    parts = to_proto(msg)
    rmsg, gmsg = call(
        functools.partial(crops_kernel, n_z, n),
        (shape((n_z, 8, 128)), shape((n, size, width), BF16)),
        (parts, totals, p_sum, student_emb),
        scratch=[vm((8, 128)), vm((128, 128))],
    )
    rmsg, g_student, *late = tie((rmsg, g_student) + gathered)
    e_own, g_late = call(
        own_teacher_kernel,
        (shape((n_z, chip, crops), BF16), shape((chip, width))),
        (prototypes,) + tuple(late) + (tot_parts,),
        specs=[HBM] * 9 + [VMEM],
        outs=(HBM, VMEM),
        scratch=[
            vm((chip, width), BF16), blocks(crops, width), vm((crops, width), BF16),
            blocks(chip, crops), sems(1), sems(n_z), sems(1), sems(n_z),
        ],
        flops=block_flops,
        limit=57,
    )
    parts = to_z(rmsg)
    parts, gmsg, e_own = tie((parts, gmsg, e_own))
    pieces = to_proto(gmsg)
    keep, give = call(
        protos_kernel,
        (shape((2 * owned + 8, width)), shape((owned + 8, width))),
        (parts, e_own, g_student, g_late, col, prototypes) + tuple(late),
        specs=[VMEM, HBM, VMEM, VMEM, VMEM, HBM] + [HBM] * 8,
        scratch=[
            vm((owned, width), BF16), blocks(chip, crops), blocks(crops, width), vm((chip, width)),
            sems(1), sems(n_z), sems(n_z),
        ],
        flops=block_flops,
        limit=57,
    )
    grad_protos, loss = call(
        functools.partial(finish_kernel, float(crops * n_dp)),
        (shape((owned, width)), shape((1, 1))),
        (keep, swap(give)),
        outs=(VMEM, SMEM),
    )
    grad_student = pieces.astype(F32).reshape(crops, width)
    return grad_student, grad_protos[None], loss[0, 0]


def solution(mesh):
    fine = Mesh(np.asarray(mesh.devices).reshape(8, 2, 4, 4), ("z", "core", "y", "x"))
    in_specs = (P(CROPS, None), P(CROPS, None), P(PROTOS, None))
    out_specs = (P(CROPS, None), P(PROTOS, CROPS, None), P())
    return jax.shard_map(
        per_device, mesh=fine, in_specs=in_specs, out_specs=out_specs, check_vma=False
    )
```

```python
import functools

import jax
import jax.numpy as jnp
import numpy as np
from jax import lax
from jax.experimental import pallas as pl
from jax.experimental.pallas import tpu as pltpu
from jax.sharding import Mesh, PartitionSpec as P

CROPS = ("z", "core")
PROTOS = ("y", "x")
LOG2E = 1.4426950408889634
T_SCALE = LOG2E / 0.07
S_SCALE = LOG2E / 0.1
F32 = jnp.float32
BF16 = jnp.bfloat16
VMEM = pl.BlockSpec(memory_space=pltpu.VMEM)
SMEM = pl.BlockSpec(memory_space=pltpu.SMEM)
HBM = pl.BlockSpec(memory_space=pltpu.HBM)
LAST = (((1,), (1,)), ((), ()))
CHUNK = 512


def inverse_norms(values):
    return lax.rsqrt(jnp.sum(values * values, axis=-1, keepdims=True) + 1e-06)


def half_unit(block):
    values = block.astype(F32)
    return (values * inverse_norms(values)).astype(BF16)


def column(row):
    return jnp.broadcast_to(row, (128, 128)).T


def lay_down(block):
    return jnp.sum(block.T, axis=0, keepdims=True)


def twice(block):
    return jnp.concatenate([block, block], axis=1)


def call(kernel, out, operands, specs=None, outs=None, scratch=(), flops=0, limit=12):
    touched = sum(x.size * x.dtype.itemsize for x in operands)
    return pl.pallas_call(
        kernel,
        out_shape=out,
        in_specs=specs or [VMEM] * len(operands),
        out_specs=outs or jax.tree.map(lambda _: VMEM, out),
        scratch_shapes=list(scratch),
        cost_estimate=pl.CostEstimate(flops=flops, bytes_accessed=touched, transcendentals=0),
        compiler_params=pltpu.CompilerParams(vmem_limit_bytes=limit << 20),
    )(*operands)


def copies(pairs, sems):
    out = [pltpu.make_async_copy(a, b, sems.at[k]) for k, (a, b) in enumerate(pairs)]
    return out


def begin(pairs, sems):
    started = copies(pairs, sems)
    for c in started:
        c.start()
    return started


def lanes(k, size=CHUNK):
    return pl.ds(k * size, size)


def dp_place():
    return lax.axis_index("z") * lax.axis_size("core") + lax.axis_index("core")


def proto_place():
    return lax.axis_index("y") * lax.axis_size("x") + lax.axis_index("x")


def halves_kernel(t_ref, s_ref, x_ref):
    x_ref[0] = half_unit(t_ref[...])
    x_ref[1] = half_unit(s_ref[...])


def teacher_kernel(n, x_ref, w_ref, sh_ref, e0, e1, wh_ref, msg_ref, sums):
    for j in range(w_ref.shape[0] // CHUNK):
        w_half = half_unit(w_ref[lanes(j), :])
        wh_ref[lanes(j), :] = w_half
        scores = lax.dot_general(x_ref[0], w_half, LAST, preferred_element_type=F32)
        expo = jnp.exp2(scores * T_SCALE)
        for i, e_ref in enumerate((e0, e1)):
            e_ref[:, lanes(j)] = expo[i * 256 : (i + 1) * 256].astype(BF16)
        part = jnp.sum(expo, axis=0, keepdims=True)
        for b in range(CHUNK // 128):
            at = j * (CHUNK // 128) + b
            sums[at : at + 1, :] = part[:, b * 128 : (b + 1) * 128]
    total = sums[...].astype(msg_ref.dtype)
    for k in range(n):
        msg_ref[k] = total
    sh_ref[...] = x_ref[1]


def student_kernel(sh_ref, wh_ref, tot_ref, p_ref, acc):
    for j in range(wh_ref.shape[0] // CHUNK):
        w_half = wh_ref[lanes(j), :]
        scores = lax.dot_general(sh_ref[...], w_half, LAST, preferred_element_type=F32)
        expo = jnp.exp2(scores * S_SCALE)
        part = sum(expo[:, b * 128 : (b + 1) * 128] for b in range(CHUNK // 128))
        prod = jnp.dot(expo.astype(BF16), w_half, preferred_element_type=F32)
        if j == 0:
            acc[...] = part
            p_ref[...] = prod
        else:
            acc[...] += part
            p_ref[...] += prod
    for i in range(4):
        tot_ref[i : i + 1, :] = lay_down(acc[lanes(i, 128), :])


def first_row_kernel(n, parts_ref, e0, e1, tot_ref, p_ref, msg_ref, c_ref):
    size = CHUNK // n
    tails = [jnp.concatenate([row, tot_ref[i : i + 1, :]], axis=1)
             for i, row in enumerate(row_sums(parts_ref, (e0, e1), c_ref))]
    tail = split_pair(jnp.concatenate(tails, axis=0))
    for k in range(n):
        msg_ref[k, 0:size, :] = p_ref[lanes(k, size), :].astype(BF16)
        msg_ref[k, size : size + 16, :] = tail


def split_pair(rows):
    high = rows.astype(BF16).astype(F32)
    zeros = jnp.zeros((8, rows.shape[1]), F32)
    return jnp.concatenate([high, rows - high, zeros], axis=0).astype(BF16)


def row_sums(parts_ref, e_refs, c_ref):
    c_ref[...] = 1.0 / jnp.sum(parts_ref[:, 0:32, :].astype(F32), axis=0)
    out = []
    for i in range(4):
        rows = lanes(i % 2, 128)
        acc = jnp.zeros((128, 128), F32)
        for b in range(32):
            part = e_refs[i // 2][rows, b * 128 : (b + 1) * 128].astype(F32)
            acc += part * c_ref[b : b + 1, :]
        out.append(lay_down(acc))
    return out


def row_kernel(n, parts_ref, e0, e1, msg_ref, c_ref):
    whole = jnp.concatenate(row_sums(parts_ref, (e0, e1), c_ref), axis=0)
    for k in range(n):
        msg_ref[k] = whole


def column_sums(scale, e_refs, row_col, out):
    for i in range(4):
        row_col[lanes(i, 128), :] = column(scale[i : i + 1])
    for b in range(32):
        acc = jnp.zeros((8, 128), F32)
        for i in range(4):
            rows = lanes(i, 128)
            part = e_refs[i // 2][lanes(i % 2, 128), b * 128 : (b + 1) * 128].astype(F32)
            prod = part * row_col[rows, :]
            acc += jnp.sum(prod.reshape(16, 8, 128), axis=0)
        out[b : b + 1, :] = jnp.sum(acc, axis=0, keepdims=True)


def first_column_kernel(n, parts_ref, e0, e1, msg_ref, tot_ref, p_ref, row_col, out):
    size = p_ref.shape[0]
    total = jnp.sum(parts_ref[...].astype(F32), axis=0)
    p_ref[...] = total[0:size]
    sums = total[size : size + 4] + total[size + 4 : size + 8]
    tot = sums[:, 128:256]
    tot_ref[...] = tot
    column_sums(1.0 / sums[:, 0:128], (e0, e1), row_col, out)
    whole = out[...].astype(BF16)
    tail = split_pair(tot)
    for k in range(n):
        msg_ref[k, 0:32, :] = whole
        msg_ref[k, 32:48, :] = tail


def column_kernel(parts_ref, e0, e1, msg_ref, row_col):
    column_sums(1.0 / jnp.sum(parts_ref[...], axis=0), (e0, e1), row_col, msg_ref)


def last_kernel(n, parts_ref, e0, e1, wh_ref, sh_ref, msg_ref, c_ref, prod, acc):
    c_ref[...] = 1.0 / jnp.sum(parts_ref[...], axis=0)
    size = CHUNK // n
    for j in range(e0.shape[1] // CHUNK):
        pieces = []
        for b in range(CHUNK // 128):
            at = j * (CHUNK // 128) + b
            span = slice(at * 128, (at + 1) * 128)
            piece = jnp.concatenate([e[:, span] for e in (e0, e1)], axis=0)
            pieces.append(piece.astype(F32) * c_ref[at : at + 1, :])
        part = sum(pieces)
        scaled = jnp.concatenate([p.astype(BF16) for p in pieces], axis=1)
        term = jnp.dot(scaled, wh_ref[lanes(j), :], preferred_element_type=F32)
        if j == 0:
            acc[...] = part
            prod[...] = term
        else:
            acc[...] += part
            prod[...] += term
    tails = []
    for i in range(4):
        rows = lanes(i, 128)
        dots = prod[rows, :] * sh_ref[rows, :].astype(F32)
        dots = (dots[:, 0:128] + dots[:, 128:256]) * 10.0
        tails.append(jnp.concatenate([lay_down(acc[rows, :]), lay_down(dots)], axis=1))
    tail = jnp.concatenate(tails + [jnp.zeros((4, 256), F32)], axis=0)
    for k in range(n):
        msg_ref[k, 0:size, :] = prod[lanes(k, size), :]
        msg_ref[k, size : size + 8, :] = tail


def pick_rows(rows_ref, col_ref, me, size):
    per = 128 // size
    col_ref[...] = column(rows_ref[pl.ds(me // per, 1), :])
    return twice(col_ref[pl.ds(pl.multiple_of((me % per) * size, 8), size), :])


def crops_kernel(
    n_z, n, parts_ref, tot_ref, p_ref, s_ref, rmsg_ref, gmsg_ref, rows_ref, col_ref
):
    size = CHUNK // n
    total = jnp.sum(parts_ref[...], axis=0)
    scale = 1.0 / total[size : size + 4, 0:128]
    tot = tot_ref[...]
    loss = jnp.sum(scale * total[size : size + 4, 128:256] - jnp.log(tot))
    whole = jnp.concatenate([scale, jnp.full((4, 128), loss, F32)], axis=0)
    for k in range(n_z):
        rmsg_ref[k] = whole
    me = proto_place()
    rows_ref[...] = jnp.concatenate([scale, 1.0 / tot], axis=0)
    r_col = pick_rows(rows_ref.at[0:4], col_ref, me, size)
    tot_col = pick_rows(rows_ref.at[4:8], col_ref, me, size)
    grad = (p_ref[...] * tot_col - r_col * total[0:size]) * 10.0
    values = s_ref[pl.ds(pl.multiple_of(me * size, 16), size), :].astype(F32)
    inverse = inverse_norms(values)
    s_unit = values * inverse
    grad = (grad - s_unit * jnp.sum(s_unit * grad, axis=-1, keepdims=True)) * inverse
    grad = grad.astype(BF16)
    for k in range(n):
        gmsg_ref[k] = grad


HOPS = (0, -1, 1, -2, 2, -3, 3, -4)


def slot_place(k):
    n_z = lax.axis_size("z")
    return lax.rem(lax.axis_index("z") + HOPS[k] + n_z, n_z)


def chip_rows(w_hbm, w_buf):
    rows = w_buf.shape[0]
    return w_hbm.at[pl.ds(pl.multiple_of(lax.axis_index("z") * rows, rows), rows), :]


def student_term(w_half, s_half, parts_ref, k):
    scores = lax.dot_general(w_half, s_half, LAST, preferred_element_type=F32)
    tail = parts_ref[slot_place(k) * 2 + lax.axis_index("core"), 32:48, :].astype(F32)
    inv = 1.0 / (tail[0:4] + tail[4:8])
    row = jnp.concatenate([inv[i : i + 1] for i in range(4)], axis=1)
    probs = (jnp.exp2(scores * S_SCALE) * row).astype(BF16)
    return jnp.dot(probs, s_half, preferred_element_type=F32)


def own_teacher_kernel(w_hbm, *refs):
    blocks = refs[:8]
    parts_ref, e_hbm, g_ref, w_buf, t_buf, s_buf, e_buf, w_sem, t_sems, s_sem, e_sems = refs[8:]
    w_copies = begin([(chip_rows(w_hbm, w_buf), w_buf)], w_sem)
    t_copies = begin([(x.at[0], t_buf.at[k]) for k, x in enumerate(blocks)], t_sems)
    s_copies = begin([(blocks[7].at[1], s_buf)], s_sem)
    e_copies = copies([(e_buf.at[k], e_hbm.at[k]) for k in range(8)], e_sems)
    w_copies[0].wait()
    w_half = half_unit(w_buf[...])
    for k in range(8):
        t_copies[k].wait()
        scores = lax.dot_general(w_half, t_buf[k], LAST, preferred_element_type=F32)
        e_buf[k] = jnp.exp2(scores * T_SCALE).astype(BF16)
        e_copies[k].start()
    s_copies[0].wait()
    g_ref[...] = student_term(w_half, s_buf[...], parts_ref, 7)
    for c in e_copies:
        c.wait()


def own_student_kernel(w_hbm, *refs):
    blocks = refs[:7]
    parts_ref, g_ref, w_buf, s_buf, total, w_sem, s_sems = refs[7:]
    w_copies = begin([(chip_rows(w_hbm, w_buf), w_buf)], w_sem)
    s_copies = begin([(x.at[1], s_buf.at[k]) for k, x in enumerate(blocks)], s_sems)
    w_copies[0].wait()
    w_half = half_unit(w_buf[...])
    for k in range(7):
        s_copies[k].wait()
        term = student_term(w_half, s_buf[k], parts_ref, k)
        if k == 0:
            total[...] = term
        else:
            total[...] += term
    g_ref[...] = total[...]


def protos_kernel(parts_ref, e_hbm, g_ref, late_ref, c_ref, w_hbm, *refs):
    blocks = refs[:8]
    keep_ref, give_ref, own_ref, e_buf, s_buf, total, w_sem, e_sems, s_sems = refs[8:]
    half = own_ref.shape[0]
    start = pl.multiple_of(dp_place() * half, half)
    w_copies = begin([(w_hbm.at[pl.ds(start, half), :], own_ref)], w_sem)
    e_copies = copies([(e_hbm.at[k], e_buf.at[k]) for k in range(8)], e_sems)
    s_copies = copies([(x.at[1], s_buf.at[k]) for k, x in enumerate(blocks)], s_sems)
    for one, two in zip(e_copies, s_copies):
        one.start()
        two.start()
    first = lax.axis_index("z") * 4
    cols = [column(c_ref[pl.ds(first + i, 1), :]) for i in range(4)]
    loss = jnp.zeros((1, 128), F32)
    for k in range(8):
        z = slot_place(k)
        row = jnp.concatenate([parts_ref[z, i : i + 1, :] for i in range(4)], axis=1)
        loss += parts_ref[z, 4:5, :]
        e_copies[k].wait()
        scaled = (e_buf[k].astype(F32) * row).astype(BF16)
        s_copies[k].wait()
        term = jnp.dot(scaled, s_buf[k], preferred_element_type=F32)
        if k == 0:
            total[...] = term
        else:
            total[...] += term
    for i in range(4):
        rows = lanes(i, 128)
        total[rows, :] = (
            g_ref[rows, :] + late_ref[rows, :] - total[rows, :] * twice(cols[i])
        ) * 10.0
    core = lax.axis_index("core")
    keep_ref[0:half, :] = total[pl.ds(pl.multiple_of(core * half, half), half), :]
    give_ref[0:half, :] = total[pl.ds(pl.multiple_of((1 - core) * half, half), half), :]
    loss = twice(jnp.broadcast_to(loss, (8, 128)))
    give_ref[half : half + 8, :] = loss
    keep_ref[half : half + 8, :] = loss
    w_copies[0].wait()
    keep_ref[half + 8 : 2 * half + 8, :] = own_ref[...].astype(F32)


def finish_kernel(count, keep_ref, got_ref, out_ref, mean_ref):
    half = out_ref.shape[0]
    values = keep_ref[half + 8 : 2 * half + 8, :]
    inverse = inverse_norms(values)
    w_unit = values * inverse
    grad = keep_ref[0:half, :] + got_ref[0:half, :]
    loss = keep_ref[half : half + 1, :] + got_ref[half : half + 1, :]
    out_ref[...] = (grad - w_unit * jnp.sum(w_unit * grad, axis=-1, keepdims=True)) * inverse
    mean_ref[0, 0] = loss[0, 0] * (-1.0 / count)


def shape(dims, dtype=F32):
    return jax.ShapeDtypeStruct(dims, dtype)


def per_device(teacher_emb, student_emb, prototypes):
    n_z = lax.axis_size("z")
    n_dp = n_z * lax.axis_size("core")
    n = lax.axis_size("y") * lax.axis_size("x")
    crops, width = teacher_emb.shape
    protos = prototypes.shape[0]
    owned = protos // n_dp
    size = crops // n
    to_dp = lambda msg: lax.all_to_all(msg, CROPS, 0, 0)
    to_proto = lambda msg: lax.all_to_all(msg, PROTOS, 0, 0)
    tie = lax.optimization_barrier
    vm = lambda dims, dtype=F32: pltpu.VMEM(dims, dtype)
    sems = lambda count: pltpu.SemaphoreType.DMA((count,))
    block_flops = 2 * crops * protos * width

    right = lambda x: lax.ppermute(x, "z", [(i, (i + 1) % n_z) for i in range(n_z)])
    left = lambda x: lax.ppermute(x, "z", [(i, (i - 1) % n_z) for i in range(n_z)])
    swap = lambda x: lax.ppermute(x, "core", [(0, 1), (1, 0)])

    here = call(halves_kernel, shape((2, crops, width), BF16), (teacher_emb, student_emb))
    a1, b1 = right(here), left(here)
    s_half, *expo, w_half, msg = call(
        functools.partial(teacher_kernel, n_dp),
        (
            shape((crops, width), BF16),
            *[shape((crops // 2, protos), BF16)] * 2, shape((protos, width), BF16),
            shape((n_dp, 32, 128), BF16),
        ),
        (here, prototypes),
        scratch=[vm((32, 128))],
        flops=block_flops,
    )
    tot_part, p_part = call(
        student_kernel,
        (shape((4, 128)), shape((crops, width))),
        (s_half, w_half),
        scratch=[vm((crops, 128))],
        flops=2 * block_flops,
    )
    msg, p_part = tie((msg, p_part))
    parts = to_dp(msg)
    msg = call(
        functools.partial(first_row_kernel, n),
        shape((n, size + 16, width), BF16),
        (parts, *expo, tot_part, p_part),
        scratch=[vm((32, 128))],
    )
    msg, a1, b1 = tie((msg, a1, b1))
    a2, b2 = right(a1), left(b1)
    parts = to_proto(msg)
    column_scratch = [vm((crops, 128)), vm((32, 128))]
    msg, totals, p_sum = call(
        functools.partial(first_column_kernel, n_dp),
        (shape((n_dp, 48, 128), BF16), shape((4, 128)), shape((size, width))),
        (parts, *expo),
        scratch=column_scratch,
    )
    tot_parts = to_dp(msg)
    msg = call(
        functools.partial(row_kernel, n),
        shape((n, 4, 128)),
        (tot_parts, *expo),
        scratch=[vm((32, 128))],
    )
    msg, a2, b2 = tie((msg, a2, b2))
    a3, b3 = right(a2), left(b2)
    parts = to_proto(msg)
    msg = call(
        column_kernel,
        shape((32, 128)),
        (parts, *expo),
        scratch=column_scratch[:1],
    )
    msg = msg + swap(msg)
    to_z = lambda msg: lax.all_to_all(msg, "z", 0, 0)
    parts = to_z(jnp.broadcast_to(msg, (n_z, 32, 128)))
    parts, a3, b3 = tie((parts, a3, b3))
    a4 = right(a3)
    gathered = (here, a1, b1, a2, b2, a3, b3, a4)
    msg, col = call(
        functools.partial(last_kernel, n),
        (shape((n, size + 8, width)), shape((32, 128))),
        (parts, *expo, w_half, s_half),
        scratch=[vm((crops, width)), vm((crops, 128))],
        flops=block_flops,
    )
    msg, *gathered = tie((msg,) + gathered[:-1])
    gathered = tuple(gathered) + (a4,)
    blocks = lambda rows, columns: vm((n_z, rows, columns), BF16)
    chip = 2 * owned
    g_student = call(
        own_student_kernel,
        shape((chip, width)),
        (prototypes,) + gathered[:-1] + (tot_parts,),
        specs=[HBM] * 8 + [VMEM],
        scratch=[
            vm((chip, width), BF16), blocks(crops, width), vm((chip, width)), sems(1), sems(n_z),
        ],
        flops=2 * block_flops,
        limit=57,
    )
    parts = to_proto(msg)
    rmsg, gmsg = call(
        functools.partial(crops_kernel, n_z, n),
        (shape((n_z, 8, 128)), shape((n, size, width), BF16)),
        (parts, totals, p_sum, student_emb),
        scratch=[vm((8, 128)), vm((128, 128))],
    )
    rmsg, g_student, *late = tie((rmsg, g_student) + gathered)
    e_own, g_late = call(
        own_teacher_kernel,
        (shape((n_z, chip, crops), BF16), shape((chip, width))),
        (prototypes,) + tuple(late) + (tot_parts,),
        specs=[HBM] * 9 + [VMEM],
        outs=(HBM, VMEM),
        scratch=[
            vm((chip, width), BF16), blocks(crops, width), vm((crops, width), BF16),
            blocks(chip, crops), sems(1), sems(n_z), sems(1), sems(n_z),
        ],
        flops=block_flops,
        limit=57,
    )
    parts = to_z(rmsg)
    parts, gmsg, e_own = tie((parts, gmsg, e_own))
    pieces = to_proto(gmsg)
    keep, give = call(
        protos_kernel,
        (shape((2 * owned + 8, width)), shape((owned + 8, width))),
        (parts, e_own, g_student, g_late, col, prototypes) + tuple(late),
        specs=[VMEM, HBM, VMEM, VMEM, VMEM, HBM] + [HBM] * 8,
        scratch=[
            vm((owned, width), BF16), blocks(chip, crops), blocks(crops, width), vm((chip, width)),
            sems(1), sems(n_z), sems(n_z),
        ],
        flops=block_flops,
        limit=57,
    )
    grad_protos, loss = call(
        functools.partial(finish_kernel, float(crops * n_dp)),
        (shape((owned, width)), shape((1, 1))),
        (keep, swap(give)),
        outs=(VMEM, SMEM),
    )
    grad_student = pieces.astype(F32).reshape(crops, width)
    return grad_student, grad_protos[None], loss[0, 0]


def solution(mesh):
    fine = Mesh(np.asarray(mesh.devices).reshape(8, 2, 4, 4), ("z", "core", "y", "x"))
    in_specs = (P(CROPS, None), P(CROPS, None), P(PROTOS, None))
    out_specs = (P(CROPS, None), P(PROTOS, CROPS, None), P())
    return jax.shard_map(
        per_device, mesh=fine, in_specs=in_specs, out_specs=out_specs, check_vma=False
    )
```

```python
import functools

import jax
import jax.numpy as jnp
import numpy as np
from jax import lax
from jax.experimental import pallas as pl
from jax.experimental.pallas import tpu as pltpu
from jax.sharding import Mesh, PartitionSpec as P

CROPS = ("z", "core")
PROTOS = ("y", "x")
LOG2E = 1.4426950408889634
T_SCALE = LOG2E / 0.07
S_SCALE = LOG2E / 0.1
F32 = jnp.float32
BF16 = jnp.bfloat16
VMEM = pl.BlockSpec(memory_space=pltpu.VMEM)
SMEM = pl.BlockSpec(memory_space=pltpu.SMEM)
HBM = pl.BlockSpec(memory_space=pltpu.HBM)
LAST = (((1,), (1,)), ((), ()))
CHUNK = 512


def inverse_norms(values):
    return lax.rsqrt(jnp.sum(values * values, axis=-1, keepdims=True) + 1e-06)


def half_unit(block):
    values = block.astype(F32)
    return (values * inverse_norms(values)).astype(BF16)


def column(row):
    return jnp.broadcast_to(row, (128, 128)).T


def lay_down(block):
    return jnp.sum(block.T, axis=0, keepdims=True)


def twice(block):
    return jnp.concatenate([block, block], axis=1)


def call(kernel, out, operands, specs=None, outs=None, scratch=(), flops=0, limit=12):
    touched = sum(x.size * x.dtype.itemsize for x in operands)
    return pl.pallas_call(
        kernel,
        out_shape=out,
        in_specs=specs or [VMEM] * len(operands),
        out_specs=outs or jax.tree.map(lambda _: VMEM, out),
        scratch_shapes=list(scratch),
        cost_estimate=pl.CostEstimate(flops=flops, bytes_accessed=touched, transcendentals=0),
        compiler_params=pltpu.CompilerParams(vmem_limit_bytes=limit << 20),
    )(*operands)


def copies(pairs, sems):
    out = [pltpu.make_async_copy(a, b, sems.at[k]) for k, (a, b) in enumerate(pairs)]
    return out


def begin(pairs, sems):
    started = copies(pairs, sems)
    for c in started:
        c.start()
    return started


def lanes(k, size=CHUNK):
    return pl.ds(k * size, size)


def dp_place():
    return lax.axis_index("z") * lax.axis_size("core") + lax.axis_index("core")


def proto_place():
    return lax.axis_index("y") * lax.axis_size("x") + lax.axis_index("x")


def halves_kernel(t_ref, s_ref, x_ref):
    x_ref[0] = half_unit(t_ref[...])
    x_ref[1] = half_unit(s_ref[...])


def teacher_kernel(n, x_ref, w_ref, sh_ref, e0, e1, wh_ref, msg_ref, sums):
    for j in range(w_ref.shape[0] // CHUNK):
        w_half = half_unit(w_ref[lanes(j), :])
        wh_ref[lanes(j), :] = w_half
        scores = lax.dot_general(x_ref[0], w_half, LAST, preferred_element_type=F32)
        expo = jnp.exp2(scores * T_SCALE)
        for i, e_ref in enumerate((e0, e1)):
            e_ref[:, lanes(j)] = expo[i * 256 : (i + 1) * 256].astype(BF16)
        part = jnp.sum(expo, axis=0, keepdims=True)
        for b in range(CHUNK // 128):
            at = j * (CHUNK // 128) + b
            sums[at : at + 1, :] = part[:, b * 128 : (b + 1) * 128]
    total = sums[...].astype(msg_ref.dtype)
    for k in range(n):
        msg_ref[k] = total
    sh_ref[...] = x_ref[1]


def student_kernel(sh_ref, wh_ref, tot_ref, p_ref, acc):
    for j in range(wh_ref.shape[0] // CHUNK):
        w_half = wh_ref[lanes(j), :]
        scores = lax.dot_general(sh_ref[...], w_half, LAST, preferred_element_type=F32)
        expo = jnp.exp2(scores * S_SCALE)
        part = sum(expo[:, b * 128 : (b + 1) * 128] for b in range(CHUNK // 128))
        prod = jnp.dot(expo.astype(BF16), w_half, preferred_element_type=F32)
        if j == 0:
            acc[...] = part
            p_ref[...] = prod
        else:
            acc[...] += part
            p_ref[...] += prod
    for i in range(4):
        tot_ref[i : i + 1, :] = lay_down(acc[lanes(i, 128), :])


def first_row_kernel(n, parts_ref, e0, e1, tot_ref, p_ref, msg_ref, c_ref):
    size = CHUNK // n
    tails = [jnp.concatenate([row, tot_ref[i : i + 1, :]], axis=1)
             for i, row in enumerate(row_sums(parts_ref, (e0, e1), c_ref))]
    tail = split_pair(jnp.concatenate(tails, axis=0))
    for k in range(n):
        msg_ref[k, 0:size, :] = p_ref[lanes(k, size), :].astype(BF16)
        msg_ref[k, size : size + 16, :] = tail


def split_pair(rows):
    high = rows.astype(BF16).astype(F32)
    zeros = jnp.zeros((8, rows.shape[1]), F32)
    return jnp.concatenate([high, rows - high, zeros], axis=0).astype(BF16)


def row_sums(parts_ref, e_refs, c_ref):
    c_ref[...] = 1.0 / jnp.sum(parts_ref[:, 0:32, :].astype(F32), axis=0)
    out = []
    for i in range(4):
        rows = lanes(i % 2, 128)
        acc = jnp.zeros((128, 128), F32)
        for b in range(32):
            part = e_refs[i // 2][rows, b * 128 : (b + 1) * 128].astype(F32)
            acc += part * c_ref[b : b + 1, :]
        out.append(lay_down(acc))
    return out


def row_kernel(n, parts_ref, e0, e1, msg_ref, c_ref):
    whole = jnp.concatenate(row_sums(parts_ref, (e0, e1), c_ref), axis=0)
    for k in range(n):
        msg_ref[k] = whole


def column_sums(scale, e_refs, row_col, out):
    for i in range(4):
        row_col[lanes(i, 128), :] = column(scale[i : i + 1])
    for b in range(32):
        acc = jnp.zeros((8, 128), F32)
        for i in range(4):
            rows = lanes(i, 128)
            part = e_refs[i // 2][lanes(i % 2, 128), b * 128 : (b + 1) * 128].astype(F32)
            prod = part * row_col[rows, :]
            acc += jnp.sum(prod.reshape(16, 8, 128), axis=0)
        out[b : b + 1, :] = jnp.sum(acc, axis=0, keepdims=True)


def first_column_kernel(n, parts_ref, e0, e1, msg_ref, tot_ref, p_ref, row_col, out):
    size = p_ref.shape[0]
    total = jnp.sum(parts_ref[...].astype(F32), axis=0)
    p_ref[...] = total[0:size]
    sums = total[size : size + 4] + total[size + 4 : size + 8]
    tot = sums[:, 128:256]
    tot_ref[...] = tot
    column_sums(1.0 / sums[:, 0:128], (e0, e1), row_col, out)
    whole = out[...].astype(BF16)
    tail = split_pair(tot)
    for k in range(n):
        msg_ref[k, 0:32, :] = whole
        msg_ref[k, 32:48, :] = tail


def column_kernel(parts_ref, e0, e1, msg_ref, row_col):
    column_sums(1.0 / jnp.sum(parts_ref[...], axis=0), (e0, e1), row_col, msg_ref)


def last_kernel(n, parts_ref, e0, e1, wh_ref, sh_ref, msg_ref, c_ref, prod, acc):
    c_ref[...] = 1.0 / jnp.sum(parts_ref[...], axis=0)
    size = CHUNK // n
    for j in range(e0.shape[1] // CHUNK):
        pieces = []
        for b in range(CHUNK // 128):
            at = j * (CHUNK // 128) + b
            span = slice(at * 128, (at + 1) * 128)
            piece = jnp.concatenate([e[:, span] for e in (e0, e1)], axis=0)
            pieces.append(piece.astype(F32) * c_ref[at : at + 1, :])
        part = sum(pieces)
        scaled = jnp.concatenate([p.astype(BF16) for p in pieces], axis=1)
        term = jnp.dot(scaled, wh_ref[lanes(j), :], preferred_element_type=F32)
        if j == 0:
            acc[...] = part
            prod[...] = term
        else:
            acc[...] += part
            prod[...] += term
    tails = []
    for i in range(4):
        rows = lanes(i, 128)
        dots = prod[rows, :] * sh_ref[rows, :].astype(F32)
        dots = (dots[:, 0:128] + dots[:, 128:256]) * 10.0
        tails.append(jnp.concatenate([lay_down(acc[rows, :]), lay_down(dots)], axis=1))
    tail = jnp.concatenate(tails + [jnp.zeros((4, 256), F32)], axis=0)
    for k in range(n):
        msg_ref[k, 0:size, :] = prod[lanes(k, size), :]
        msg_ref[k, size : size + 8, :] = tail


def pick_rows(rows_ref, col_ref, me, size):
    per = 128 // size
    col_ref[...] = column(rows_ref[pl.ds(me // per, 1), :])
    return twice(col_ref[pl.ds(pl.multiple_of((me % per) * size, 8), size), :])


def crops_kernel(
    n_z, n, parts_ref, tot_ref, p_ref, s_ref, rmsg_ref, gmsg_ref, rows_ref, col_ref
):
    size = CHUNK // n
    total = jnp.sum(parts_ref[...], axis=0)
    scale = 1.0 / total[size : size + 4, 0:128]
    tot = tot_ref[...]
    loss = jnp.sum(scale * total[size : size + 4, 128:256] - jnp.log(tot))
    whole = jnp.concatenate([scale, jnp.full((4, 128), loss, F32)], axis=0)
    for k in range(n_z):
        rmsg_ref[k] = whole
    me = proto_place()
    rows_ref[...] = jnp.concatenate([scale, 1.0 / tot], axis=0)
    r_col = pick_rows(rows_ref.at[0:4], col_ref, me, size)
    tot_col = pick_rows(rows_ref.at[4:8], col_ref, me, size)
    grad = (p_ref[...] * tot_col - r_col * total[0:size]) * 10.0
    values = s_ref[pl.ds(pl.multiple_of(me * size, 16), size), :].astype(F32)
    inverse = inverse_norms(values)
    s_unit = values * inverse
    grad = (grad - s_unit * jnp.sum(s_unit * grad, axis=-1, keepdims=True)) * inverse
    grad = grad.astype(BF16)
    for k in range(n):
        gmsg_ref[k] = grad


EARLY = 2
HOPS = (0, -1, 1, -2, 2, -3, 3, -4)


def slot_place(k):
    n_z = lax.axis_size("z")
    return lax.rem(lax.axis_index("z") + HOPS[k] + n_z, n_z)


def chip_rows(w_hbm, w_buf):
    rows = w_buf.shape[0]
    return w_hbm.at[pl.ds(pl.multiple_of(lax.axis_index("z") * rows, rows), rows), :]


def student_term(w_half, s_half, parts_ref, k):
    scores = lax.dot_general(w_half, s_half, LAST, preferred_element_type=F32)
    tail = parts_ref[slot_place(k) * 2 + lax.axis_index("core"), 32:48, :].astype(F32)
    inv = 1.0 / (tail[0:4] + tail[4:8])
    row = jnp.concatenate([inv[i : i + 1] for i in range(4)], axis=1)
    probs = (jnp.exp2(scores * S_SCALE) * row).astype(BF16)
    return jnp.dot(probs, s_half, preferred_element_type=F32)


def teacher_term(w_half, t_half):
    scores = lax.dot_general(w_half, t_half, LAST, preferred_element_type=F32)
    return jnp.exp2(scores * T_SCALE).astype(BF16)


def own_teacher_kernel(w_hbm, *refs):
    late = 8 - EARLY
    blocks = refs[:late]
    parts_ref, e_hbm, g_ref, w_buf, t_buf, s_buf, e_buf, w_sem, t_sems, s_sem, e_sems = refs[late:]
    w_copies = begin([(chip_rows(w_hbm, w_buf), w_buf)], w_sem)
    t_copies = begin([(x.at[0], t_buf.at[k]) for k, x in enumerate(blocks)], t_sems)
    s_copies = begin([(blocks[-1].at[1], s_buf)], s_sem)
    e_copies = copies([(e_buf.at[k], e_hbm.at[k]) for k in range(late)], e_sems)
    w_copies[0].wait()
    w_half = half_unit(w_buf[...])
    for k in range(late):
        t_copies[k].wait()
        e_buf[k] = teacher_term(w_half, t_buf[k])
        e_copies[k].start()
    s_copies[0].wait()
    g_ref[...] = student_term(w_half, s_buf[...], parts_ref, 7)
    for c in e_copies:
        c.wait()


def own_student_kernel(w_hbm, *refs):
    blocks = refs[:7]
    parts_ref, e_hbm, g_ref, w_buf, s_buf, t_buf, e_buf, total, w_sem, s_sems, t_sems, e_sems = refs[7:]
    w_copies = begin([(chip_rows(w_hbm, w_buf), w_buf)], w_sem)
    t_copies = begin([(blocks[k].at[0], t_buf.at[k]) for k in range(EARLY)], t_sems)
    s_copies = begin([(x.at[1], s_buf.at[k]) for k, x in enumerate(blocks)], s_sems)
    e_copies = copies([(e_buf.at[k], e_hbm.at[k]) for k in range(EARLY)], e_sems)
    w_copies[0].wait()
    w_half = half_unit(w_buf[...])
    for k in range(EARLY):
        t_copies[k].wait()
        e_buf[k] = teacher_term(w_half, t_buf[k])
        e_copies[k].start()
    for k in range(7):
        s_copies[k].wait()
        term = student_term(w_half, s_buf[k], parts_ref, k)
        if k == 0:
            total[...] = term
        else:
            total[...] += term
    g_ref[...] = total[...]
    for c in e_copies:
        c.wait()


def protos_kernel(parts_ref, early_hbm, e_hbm, g_ref, late_ref, col_parts_ref, w_hbm, *refs):
    blocks = refs[:8]
    keep_ref, give_ref, own_ref, c_ref, e_buf, s_buf, total, w_sem, e_sems, s_sems = refs[8:]
    half = own_ref.shape[0]
    start = pl.multiple_of(dp_place() * half, half)
    w_copies = begin([(w_hbm.at[pl.ds(start, half), :], own_ref)], w_sem)
    e_pairs = [(early_hbm.at[k], e_buf.at[k]) for k in range(EARLY)]
    e_pairs += [(e_hbm.at[k - EARLY], e_buf.at[k]) for k in range(EARLY, 8)]
    e_copies = copies(e_pairs, e_sems)
    s_copies = copies([(x.at[1], s_buf.at[k]) for k, x in enumerate(blocks)], s_sems)
    for one, two in zip(e_copies, s_copies):
        one.start()
        two.start()
    c_ref[...] = 1.0 / jnp.sum(col_parts_ref[...], axis=0)
    first = lax.axis_index("z") * 4
    cols = [column(c_ref[pl.ds(first + i, 1), :]) for i in range(4)]
    loss = jnp.zeros((1, 128), F32)
    for k in range(8):
        z = slot_place(k)
        row = jnp.concatenate([parts_ref[z, i : i + 1, :] for i in range(4)], axis=1)
        loss += parts_ref[z, 4:5, :]
        e_copies[k].wait()
        scaled = (e_buf[k].astype(F32) * row).astype(BF16)
        s_copies[k].wait()
        term = jnp.dot(scaled, s_buf[k], preferred_element_type=F32)
        if k == 0:
            total[...] = term
        else:
            total[...] += term
    for i in range(4):
        rows = lanes(i, 128)
        total[rows, :] = (
            g_ref[rows, :] + late_ref[rows, :] - total[rows, :] * twice(cols[i])
        ) * 10.0
    core = lax.axis_index("core")
    keep_ref[0:half, :] = total[pl.ds(pl.multiple_of(core * half, half), half), :]
    give_ref[0:half, :] = total[pl.ds(pl.multiple_of((1 - core) * half, half), half), :]
    loss = twice(jnp.broadcast_to(loss, (8, 128)))
    give_ref[half : half + 8, :] = loss
    keep_ref[half : half + 8, :] = loss
    w_copies[0].wait()
    keep_ref[half + 8 : 2 * half + 8, :] = own_ref[...].astype(F32)


def finish_kernel(count, keep_ref, got_ref, out_ref, mean_ref):
    half = out_ref.shape[0]
    values = keep_ref[half + 8 : 2 * half + 8, :]
    inverse = inverse_norms(values)
    w_unit = values * inverse
    grad = keep_ref[0:half, :] + got_ref[0:half, :]
    loss = keep_ref[half : half + 1, :] + got_ref[half : half + 1, :]
    out_ref[...] = (grad - w_unit * jnp.sum(w_unit * grad, axis=-1, keepdims=True)) * inverse
    mean_ref[0, 0] = loss[0, 0] * (-1.0 / count)


def shape(dims, dtype=F32):
    return jax.ShapeDtypeStruct(dims, dtype)


def per_device(teacher_emb, student_emb, prototypes):
    n_z = lax.axis_size("z")
    n_dp = n_z * lax.axis_size("core")
    n = lax.axis_size("y") * lax.axis_size("x")
    crops, width = teacher_emb.shape
    protos = prototypes.shape[0]
    owned = protos // n_dp
    size = crops // n
    to_dp = lambda msg: lax.all_to_all(msg, CROPS, 0, 0)
    to_proto = lambda msg: lax.all_to_all(msg, PROTOS, 0, 0)
    tie = lax.optimization_barrier
    vm = lambda dims, dtype=F32: pltpu.VMEM(dims, dtype)
    sems = lambda count: pltpu.SemaphoreType.DMA((count,))
    block_flops = 2 * crops * protos * width

    right = lambda x: lax.ppermute(x, "z", [(i, (i + 1) % n_z) for i in range(n_z)])
    left = lambda x: lax.ppermute(x, "z", [(i, (i - 1) % n_z) for i in range(n_z)])
    swap = lambda x: lax.ppermute(x, "core", [(0, 1), (1, 0)])

    here = call(halves_kernel, shape((2, crops, width), BF16), (teacher_emb, student_emb))
    a1, b1 = right(here), left(here)
    s_half, *expo, w_half, msg = call(
        functools.partial(teacher_kernel, n_dp),
        (
            shape((crops, width), BF16),
            *[shape((crops // 2, protos), BF16)] * 2, shape((protos, width), BF16),
            shape((n_dp, 32, 128), BF16),
        ),
        (here, prototypes),
        scratch=[vm((32, 128))],
        flops=block_flops,
    )
    tot_part, p_part = call(
        student_kernel,
        (shape((4, 128)), shape((crops, width))),
        (s_half, w_half),
        scratch=[vm((crops, 128))],
        flops=2 * block_flops,
    )
    msg, p_part = tie((msg, p_part))
    parts = to_dp(msg)
    msg = call(
        functools.partial(first_row_kernel, n),
        shape((n, size + 16, width), BF16),
        (parts, *expo, tot_part, p_part),
        scratch=[vm((32, 128))],
    )
    msg, a1, b1 = tie((msg, a1, b1))
    a2, b2 = right(a1), left(b1)
    parts = to_proto(msg)
    column_scratch = [vm((crops, 128)), vm((32, 128))]
    msg, totals, p_sum = call(
        functools.partial(first_column_kernel, n_dp),
        (shape((n_dp, 48, 128), BF16), shape((4, 128)), shape((size, width))),
        (parts, *expo),
        scratch=column_scratch,
    )
    tot_parts = to_dp(msg)
    msg = call(
        functools.partial(row_kernel, n),
        shape((n, 4, 128)),
        (tot_parts, *expo),
        scratch=[vm((32, 128))],
    )
    msg, a2, b2 = tie((msg, a2, b2))
    a3, b3 = right(a2), left(b2)
    parts = to_proto(msg)
    msg = call(
        column_kernel,
        shape((32, 128)),
        (parts, *expo),
        scratch=column_scratch[:1],
    )
    msg = msg + swap(msg)
    to_z = lambda msg: lax.all_to_all(msg, "z", 0, 0)
    parts = to_z(jnp.broadcast_to(msg, (n_z, 32, 128)))
    parts, a3, b3 = tie((parts, a3, b3))
    col_parts = parts
    a4 = right(a3)
    gathered = (here, a1, b1, a2, b2, a3, b3, a4)
    msg = call(
        functools.partial(last_kernel, n),
        shape((n, size + 8, width)),
        (parts, *expo, w_half, s_half),
        scratch=[vm((32, 128)), vm((crops, width)), vm((crops, 128))],
        flops=block_flops,
    )
    msg, *gathered = tie((msg,) + gathered[:-1])
    gathered = tuple(gathered) + (a4,)
    blocks = lambda rows, columns: vm((n_z, rows, columns), BF16)
    chip = 2 * owned
    e_early, g_student = call(
        own_student_kernel,
        (shape((EARLY, chip, crops), BF16), shape((chip, width))),
        (prototypes,) + gathered[:-1] + (tot_parts,),
        specs=[HBM] * 8 + [VMEM],
        outs=(HBM, VMEM),
        scratch=[
            vm((chip, width), BF16), blocks(crops, width), vm((EARLY, crops, width), BF16),
            vm((EARLY, chip, crops), BF16), vm((chip, width)),
            sems(1), sems(n_z), sems(EARLY), sems(EARLY),
        ],
        flops=2 * block_flops,
        limit=57,
    )
    parts = to_proto(msg)
    rmsg, gmsg = call(
        functools.partial(crops_kernel, n_z, n),
        (shape((n_z, 8, 128)), shape((n, size, width), BF16)),
        (parts, totals, p_sum, student_emb),
        scratch=[vm((8, 128)), vm((128, 128))],
    )
    rmsg, g_student, *late = tie((rmsg, g_student) + gathered)
    e_own, g_late = call(
        own_teacher_kernel,
        (shape((n_z - EARLY, chip, crops), BF16), shape((chip, width))),
        (prototypes,) + tuple(late)[EARLY:] + (tot_parts,),
        specs=[HBM] * (9 - EARLY) + [VMEM],
        outs=(HBM, VMEM),
        scratch=[
            vm((chip, width), BF16), vm((n_z - EARLY, crops, width), BF16),
            vm((crops, width), BF16), vm((n_z - EARLY, chip, crops), BF16),
            sems(1), sems(n_z - EARLY), sems(1), sems(n_z - EARLY),
        ],
        flops=block_flops,
        limit=57,
    )
    parts = to_z(rmsg)
    parts, gmsg, e_own = tie((parts, gmsg, e_own))
    pieces = to_proto(gmsg)
    keep, give = call(
        protos_kernel,
        (shape((2 * owned + 8, width)), shape((owned + 8, width))),
        (parts, e_early, e_own, g_student, g_late, col_parts, prototypes) + tuple(late),
        specs=[VMEM, HBM, HBM, VMEM, VMEM, VMEM, HBM] + [HBM] * 8,
        scratch=[
            vm((owned, width), BF16), vm((32, 128)), blocks(chip, crops), blocks(crops, width), vm((chip, width)),
            sems(1), sems(n_z), sems(n_z),
        ],
        flops=block_flops,
        limit=57,
    )
    grad_protos, loss = call(
        functools.partial(finish_kernel, float(crops * n_dp)),
        (shape((owned, width)), shape((1, 1))),
        (keep, swap(give)),
        outs=(VMEM, SMEM),
    )
    grad_student = pieces.astype(F32).reshape(crops, width)
    return grad_student, grad_protos[None], loss[0, 0]


def solution(mesh):
    fine = Mesh(np.asarray(mesh.devices).reshape(8, 2, 4, 4), ("z", "core", "y", "x"))
    in_specs = (P(CROPS, None), P(CROPS, None), P(PROTOS, None))
    out_specs = (P(CROPS, None), P(PROTOS, CROPS, None), P())
    return jax.shard_map(
        per_device, mesh=fine, in_specs=in_specs, out_specs=out_specs, check_vma=False
    )
```

```python
import functools

import jax
import jax.numpy as jnp
import numpy as np
from jax import lax
from jax.experimental import pallas as pl
from jax.experimental.pallas import tpu as pltpu
from jax.sharding import Mesh, PartitionSpec as P

CROPS = ("z", "core")
PROTOS = ("y", "x")
LOG2E = 1.4426950408889634
T_SCALE = LOG2E / 0.07
S_SCALE = LOG2E / 0.1
F32 = jnp.float32
BF16 = jnp.bfloat16
VMEM = pl.BlockSpec(memory_space=pltpu.VMEM)
SMEM = pl.BlockSpec(memory_space=pltpu.SMEM)
HBM = pl.BlockSpec(memory_space=pltpu.HBM)
LAST = (((1,), (1,)), ((), ()))
CHUNK = 512


def inverse_norms(values):
    return lax.rsqrt(jnp.sum(values * values, axis=-1, keepdims=True) + 1e-06)


def half_unit(block):
    values = block.astype(F32)
    return (values * inverse_norms(values)).astype(BF16)


def column(row):
    return jnp.broadcast_to(row, (128, 128)).T


def lay_down(block):
    return jnp.sum(block.T, axis=0, keepdims=True)


def twice(block):
    return jnp.concatenate([block, block], axis=1)


def call(kernel, out, operands, specs=None, outs=None, scratch=(), flops=0, limit=12):
    touched = sum(x.size * x.dtype.itemsize for x in operands)
    return pl.pallas_call(
        kernel,
        out_shape=out,
        in_specs=specs or [VMEM] * len(operands),
        out_specs=outs or jax.tree.map(lambda _: VMEM, out),
        scratch_shapes=list(scratch),
        cost_estimate=pl.CostEstimate(flops=flops, bytes_accessed=touched, transcendentals=0),
        compiler_params=pltpu.CompilerParams(vmem_limit_bytes=limit << 20),
    )(*operands)


def copies(pairs, sems):
    out = [pltpu.make_async_copy(a, b, sems.at[k]) for k, (a, b) in enumerate(pairs)]
    return out


def begin(pairs, sems):
    started = copies(pairs, sems)
    for c in started:
        c.start()
    return started


def lanes(k, size=CHUNK):
    return pl.ds(k * size, size)


def dp_place():
    return lax.axis_index("z") * lax.axis_size("core") + lax.axis_index("core")


def proto_place():
    return lax.axis_index("y") * lax.axis_size("x") + lax.axis_index("x")


def halves_kernel(t_ref, s_ref, x_ref):
    x_ref[0] = half_unit(t_ref[...])
    x_ref[1] = half_unit(s_ref[...])


def teacher_kernel(n, x_ref, w_ref, sh_ref, e0, e1, wh_ref, msg_ref, sums):
    for j in range(w_ref.shape[0] // CHUNK):
        w_half = half_unit(w_ref[lanes(j), :])
        wh_ref[lanes(j), :] = w_half
        scores = lax.dot_general(x_ref[0], w_half, LAST, preferred_element_type=F32)
        expo = jnp.exp2(scores * T_SCALE)
        for i, e_ref in enumerate((e0, e1)):
            e_ref[:, lanes(j)] = expo[i * 256 : (i + 1) * 256].astype(BF16)
        part = jnp.sum(expo, axis=0, keepdims=True)
        for b in range(CHUNK // 128):
            at = j * (CHUNK // 128) + b
            sums[at : at + 1, :] = part[:, b * 128 : (b + 1) * 128]
    total = sums[...].astype(msg_ref.dtype)
    for k in range(n):
        msg_ref[k] = total
    sh_ref[...] = x_ref[1]


def student_kernel(sh_ref, wh_ref, tot_ref, p_ref, acc):
    for j in range(wh_ref.shape[0] // CHUNK):
        w_half = wh_ref[lanes(j), :]
        scores = lax.dot_general(sh_ref[...], w_half, LAST, preferred_element_type=F32)
        expo = jnp.exp2(scores * S_SCALE)
        part = sum(expo[:, b * 128 : (b + 1) * 128] for b in range(CHUNK // 128))
        prod = jnp.dot(expo.astype(BF16), w_half, preferred_element_type=F32)
        if j == 0:
            acc[...] = part
            p_ref[...] = prod
        else:
            acc[...] += part
            p_ref[...] += prod
    for i in range(4):
        tot_ref[i : i + 1, :] = lay_down(acc[lanes(i, 128), :])


def first_row_kernel(n, parts_ref, e0, e1, tot_ref, p_ref, msg_ref, c_ref):
    size = CHUNK // n
    tails = [jnp.concatenate([row, tot_ref[i : i + 1, :]], axis=1)
             for i, row in enumerate(row_sums(parts_ref, (e0, e1), c_ref))]
    tail = split_pair(jnp.concatenate(tails, axis=0))
    for k in range(n):
        msg_ref[k, 0:size, :] = p_ref[lanes(k, size), :].astype(BF16)
        msg_ref[k, size : size + 16, :] = tail


def split_pair(rows):
    high = rows.astype(BF16).astype(F32)
    zeros = jnp.zeros((8, rows.shape[1]), F32)
    return jnp.concatenate([high, rows - high, zeros], axis=0).astype(BF16)


def row_sums(parts_ref, e_refs, c_ref):
    c_ref[...] = 1.0 / jnp.sum(parts_ref[:, 0:32, :].astype(F32), axis=0)
    out = []
    for i in range(4):
        rows = lanes(i % 2, 128)
        acc = jnp.zeros((128, 128), F32)
        for b in range(32):
            part = e_refs[i // 2][rows, b * 128 : (b + 1) * 128].astype(F32)
            acc += part * c_ref[b : b + 1, :]
        out.append(lay_down(acc))
    return out


def row_kernel(n, parts_ref, e0, e1, msg_ref, c_ref):
    whole = jnp.concatenate(row_sums(parts_ref, (e0, e1), c_ref), axis=0)
    for k in range(n):
        msg_ref[k] = whole


def column_sums(scale, e_refs, row_col, out):
    for i in range(4):
        row_col[lanes(i, 128), :] = column(scale[i : i + 1])
    for b in range(32):
        acc = jnp.zeros((8, 128), F32)
        for i in range(4):
            rows = lanes(i, 128)
            part = e_refs[i // 2][lanes(i % 2, 128), b * 128 : (b + 1) * 128].astype(F32)
            prod = part * row_col[rows, :]
            acc += jnp.sum(prod.reshape(16, 8, 128), axis=0)
        out[b : b + 1, :] = jnp.sum(acc, axis=0, keepdims=True)


def first_column_kernel(n, parts_ref, e0, e1, msg_ref, tot_ref, p_ref, row_col, out):
    size = p_ref.shape[0]
    total = jnp.sum(parts_ref[...].astype(F32), axis=0)
    p_ref[...] = total[0:size]
    sums = total[size : size + 4] + total[size + 4 : size + 8]
    tot = sums[:, 128:256]
    tot_ref[...] = tot
    column_sums(1.0 / sums[:, 0:128], (e0, e1), row_col, out)
    whole = out[...].astype(BF16)
    tail = split_pair(tot)
    for k in range(n):
        msg_ref[k, 0:32, :] = whole
        msg_ref[k, 32:48, :] = tail


def column_kernel(parts_ref, e0, e1, msg_ref, row_col):
    column_sums(1.0 / jnp.sum(parts_ref[...], axis=0), (e0, e1), row_col, msg_ref)


def last_kernel(n, parts_ref, e0, e1, wh_ref, sh_ref, msg_ref, c_ref, prod, acc):
    c_ref[...] = 1.0 / jnp.sum(parts_ref[...], axis=0)
    size = CHUNK // n
    for j in range(e0.shape[1] // CHUNK):
        pieces = []
        for b in range(CHUNK // 128):
            at = j * (CHUNK // 128) + b
            span = slice(at * 128, (at + 1) * 128)
            piece = jnp.concatenate([e[:, span] for e in (e0, e1)], axis=0)
            pieces.append(piece.astype(F32) * c_ref[at : at + 1, :])
        part = sum(pieces)
        scaled = jnp.concatenate([p.astype(BF16) for p in pieces], axis=1)
        term = jnp.dot(scaled, wh_ref[lanes(j), :], preferred_element_type=F32)
        if j == 0:
            acc[...] = part
            prod[...] = term
        else:
            acc[...] += part
            prod[...] += term
    tails = []
    for i in range(4):
        rows = lanes(i, 128)
        dots = prod[rows, :] * sh_ref[rows, :].astype(F32)
        dots = (dots[:, 0:128] + dots[:, 128:256]) * 10.0
        tails.append(jnp.concatenate([lay_down(acc[rows, :]), lay_down(dots)], axis=1))
    tail = jnp.concatenate(tails + [jnp.zeros((4, 256), F32)], axis=0)
    for k in range(n):
        msg_ref[k, 0:size, :] = prod[lanes(k, size), :]
        msg_ref[k, size : size + 8, :] = tail


def pick_rows(rows_ref, col_ref, me, size):
    per = 128 // size
    col_ref[...] = column(rows_ref[pl.ds(me // per, 1), :])
    return twice(col_ref[pl.ds(pl.multiple_of((me % per) * size, 8), size), :])


def crops_kernel(
    n_z, n, parts_ref, tot_ref, p_ref, s_ref, rmsg_ref, gmsg_ref, rows_ref, col_ref
):
    size = CHUNK // n
    total = jnp.sum(parts_ref[...], axis=0)
    scale = 1.0 / total[size : size + 4, 0:128]
    tot = tot_ref[...]
    loss = jnp.sum(scale * total[size : size + 4, 128:256] - jnp.log(tot))
    whole = jnp.concatenate([scale, jnp.full((4, 128), loss, F32)], axis=0)
    for k in range(n_z):
        rmsg_ref[k] = whole
    me = proto_place()
    rows_ref[...] = jnp.concatenate([scale, 1.0 / tot], axis=0)
    r_col = pick_rows(rows_ref.at[0:4], col_ref, me, size)
    tot_col = pick_rows(rows_ref.at[4:8], col_ref, me, size)
    grad = (p_ref[...] * tot_col - r_col * total[0:size]) * 10.0
    values = s_ref[pl.ds(pl.multiple_of(me * size, 16), size), :].astype(F32)
    inverse = inverse_norms(values)
    s_unit = values * inverse
    grad = (grad - s_unit * jnp.sum(s_unit * grad, axis=-1, keepdims=True)) * inverse
    grad = grad.astype(BF16)
    for k in range(n):
        gmsg_ref[k] = grad


EARLY = 2
HOPS = (0, -1, 1, -2, 2, -3, 3, -4)


def slot_place(k):
    n_z = lax.axis_size("z")
    return lax.rem(lax.axis_index("z") + HOPS[k] + n_z, n_z)


def chip_rows(w_hbm, w_buf):
    rows = w_buf.shape[0]
    return w_hbm.at[pl.ds(pl.multiple_of(lax.axis_index("z") * rows, rows), rows), :]


def student_term(w_half, s_half, parts_ref, k):
    scores = lax.dot_general(w_half, s_half, LAST, preferred_element_type=F32)
    tail = parts_ref[slot_place(k) * 2 + lax.axis_index("core"), 32:48, :].astype(F32)
    inv = 1.0 / (tail[0:4] + tail[4:8])
    row = jnp.concatenate([inv[i : i + 1] for i in range(4)], axis=1)
    probs = (jnp.exp2(scores * S_SCALE) * row).astype(BF16)
    return jnp.dot(probs, s_half, preferred_element_type=F32)


def teacher_term(w_half, t_half):
    scores = lax.dot_general(w_half, t_half, LAST, preferred_element_type=F32)
    return jnp.exp2(scores * T_SCALE).astype(BF16)


def own_teacher_kernel(w_hbm, *refs):
    late = 8 - EARLY
    blocks = refs[:late]
    parts_ref, e_hbm, g_ref, w_buf, t_buf, s_buf, e_buf, w_sem, t_sems, s_sem, e_sems = refs[late:]
    w_copies = begin([(chip_rows(w_hbm, w_buf), w_buf)], w_sem)
    t_copies = begin([(x.at[0], t_buf.at[k]) for k, x in enumerate(blocks)], t_sems)
    s_copies = begin([(blocks[-1].at[1], s_buf)], s_sem)
    e_copies = copies([(e_buf.at[k], e_hbm.at[k]) for k in range(late)], e_sems)
    w_copies[0].wait()
    w_half = half_unit(w_buf[...])
    for k in range(late):
        t_copies[k].wait()
        e_buf[k] = teacher_term(w_half, t_buf[k])
        e_copies[k].start()
    s_copies[0].wait()
    g_ref[...] = student_term(w_half, s_buf[...], parts_ref, 7)
    for c in e_copies:
        c.wait()


def own_student_kernel(w_hbm, *refs):
    blocks = refs[:7]
    parts_ref, e_hbm, g_ref, w_buf, s_buf, t_buf, e_buf, total, w_sem, s_sems, t_sems, e_sems = refs[7:]
    w_copies = begin([(chip_rows(w_hbm, w_buf), w_buf)], w_sem)
    t_copies = begin([(blocks[k].at[0], t_buf.at[k]) for k in range(EARLY)], t_sems)
    s_copies = begin([(x.at[1], s_buf.at[k]) for k, x in enumerate(blocks)], s_sems)
    e_copies = copies([(e_buf.at[k], e_hbm.at[k]) for k in range(EARLY)], e_sems)
    w_copies[0].wait()
    w_half = half_unit(w_buf[...])
    for k in range(EARLY):
        t_copies[k].wait()
        e_buf[k] = teacher_term(w_half, t_buf[k])
        e_copies[k].start()
    for k in range(7):
        s_copies[k].wait()
        term = student_term(w_half, s_buf[k], parts_ref, k)
        if k == 0:
            total[...] = term
        else:
            total[...] += term
    g_ref[...] = total[...]
    for c in e_copies:
        c.wait()


def protos_kernel(parts_ref, early_hbm, e_hbm, g_ref, late_ref, col_parts_ref, w_hbm, *refs):
    blocks = refs[:8]
    keep_ref, give_ref, own_ref, c_ref, e_buf, s_buf, total, w_sem, e_sems, s_sems = refs[8:]
    half = own_ref.shape[0] // 2
    w_copies = begin([(chip_rows(w_hbm, own_ref), own_ref)], w_sem)
    e_pairs = [(early_hbm.at[k], e_buf.at[k]) for k in range(EARLY)]
    e_pairs += [(e_hbm.at[k - EARLY], e_buf.at[k]) for k in range(EARLY, 8)]
    e_copies = copies(e_pairs, e_sems)
    s_copies = copies([(x.at[1], s_buf.at[k]) for k, x in enumerate(blocks)], s_sems)
    for one, two in zip(e_copies, s_copies):
        one.start()
        two.start()
    c_ref[...] = 1.0 / jnp.sum(col_parts_ref[...], axis=0)
    first = lax.axis_index("z") * 4
    cols = [column(c_ref[pl.ds(first + i, 1), :]) for i in range(4)]
    loss = jnp.zeros((1, 128), F32)
    for k in range(8):
        z = slot_place(k)
        row = jnp.concatenate([parts_ref[z, i : i + 1, :] for i in range(4)], axis=1)
        loss += parts_ref[z, 4:5, :]
        e_copies[k].wait()
        scaled = (e_buf[k].astype(F32) * row).astype(BF16)
        s_copies[k].wait()
        term = jnp.dot(scaled, s_buf[k], preferred_element_type=F32)
        if k == 0:
            total[...] = term
        else:
            total[...] += term
    for i in range(4):
        rows = lanes(i, 128)
        grad = (g_ref[rows, :] + late_ref[rows, :] - total[rows, :] * twice(cols[i])) * 10.0
        if i == 0:
            w_copies[0].wait()
        values = own_ref[rows, :].astype(F32)
        inverse = inverse_norms(values)
        w_unit = values * inverse
        grad = (grad - w_unit * jnp.sum(w_unit * grad, axis=-1, keepdims=True)) * inverse
        total[rows, :] = grad
    core = lax.axis_index("core")
    keep_ref[0:half, :] = total[pl.ds(pl.multiple_of(core * half, half), half), :]
    give_ref[0:half, :] = total[pl.ds(pl.multiple_of((1 - core) * half, half), half), :]
    loss = twice(jnp.broadcast_to(loss, (8, 128)))
    give_ref[half : half + 8, :] = loss
    keep_ref[half : half + 8, :] = loss


def shape(dims, dtype=F32):
    return jax.ShapeDtypeStruct(dims, dtype)


def per_device(teacher_emb, student_emb, prototypes):
    n_z = lax.axis_size("z")
    n_dp = n_z * lax.axis_size("core")
    n = lax.axis_size("y") * lax.axis_size("x")
    crops, width = teacher_emb.shape
    protos = prototypes.shape[0]
    owned = protos // n_dp
    size = crops // n
    to_dp = lambda msg: lax.all_to_all(msg, CROPS, 0, 0)
    to_proto = lambda msg: lax.all_to_all(msg, PROTOS, 0, 0)
    tie = lax.optimization_barrier
    vm = lambda dims, dtype=F32: pltpu.VMEM(dims, dtype)
    sems = lambda count: pltpu.SemaphoreType.DMA((count,))
    block_flops = 2 * crops * protos * width

    right = lambda x: lax.ppermute(x, "z", [(i, (i + 1) % n_z) for i in range(n_z)])
    left = lambda x: lax.ppermute(x, "z", [(i, (i - 1) % n_z) for i in range(n_z)])
    swap = lambda x: lax.ppermute(x, "core", [(0, 1), (1, 0)])

    here = call(halves_kernel, shape((2, crops, width), BF16), (teacher_emb, student_emb))
    a1, b1 = right(here), left(here)
    s_half, *expo, w_half, msg = call(
        functools.partial(teacher_kernel, n_dp),
        (
            shape((crops, width), BF16),
            *[shape((crops // 2, protos), BF16)] * 2, shape((protos, width), BF16),
            shape((n_dp, 32, 128), BF16),
        ),
        (here, prototypes),
        scratch=[vm((32, 128))],
        flops=block_flops,
    )
    tot_part, p_part = call(
        student_kernel,
        (shape((4, 128)), shape((crops, width))),
        (s_half, w_half),
        scratch=[vm((crops, 128))],
        flops=2 * block_flops,
    )
    msg, p_part = tie((msg, p_part))
    parts = to_dp(msg)
    msg = call(
        functools.partial(first_row_kernel, n),
        shape((n, size + 16, width), BF16),
        (parts, *expo, tot_part, p_part),
        scratch=[vm((32, 128))],
    )
    msg, a1, b1 = tie((msg, a1, b1))
    a2, b2 = right(a1), left(b1)
    parts = to_proto(msg)
    column_scratch = [vm((crops, 128)), vm((32, 128))]
    msg, totals, p_sum = call(
        functools.partial(first_column_kernel, n_dp),
        (shape((n_dp, 48, 128), BF16), shape((4, 128)), shape((size, width))),
        (parts, *expo),
        scratch=column_scratch,
    )
    tot_parts = to_dp(msg)
    msg = call(
        functools.partial(row_kernel, n),
        shape((n, 4, 128)),
        (tot_parts, *expo),
        scratch=[vm((32, 128))],
    )
    msg, a2, b2 = tie((msg, a2, b2))
    a3, b3 = right(a2), left(b2)
    parts = to_proto(msg)
    msg = call(
        column_kernel,
        shape((32, 128)),
        (parts, *expo),
        scratch=column_scratch[:1],
    )
    msg = msg + swap(msg)
    to_z = lambda msg: lax.all_to_all(msg, "z", 0, 0)
    parts = to_z(jnp.broadcast_to(msg, (n_z, 32, 128)))
    parts, a3, b3 = tie((parts, a3, b3))
    col_parts = parts
    a4 = right(a3)
    gathered = (here, a1, b1, a2, b2, a3, b3, a4)
    msg = call(
        functools.partial(last_kernel, n),
        shape((n, size + 8, width)),
        (parts, *expo, w_half, s_half),
        scratch=[vm((32, 128)), vm((crops, width)), vm((crops, 128))],
        flops=block_flops,
    )
    msg, *gathered = tie((msg,) + gathered[:-1])
    gathered = tuple(gathered) + (a4,)
    blocks = lambda rows, columns: vm((n_z, rows, columns), BF16)
    chip = 2 * owned
    e_early, g_student = call(
        own_student_kernel,
        (shape((EARLY, chip, crops), BF16), shape((chip, width))),
        (prototypes,) + gathered[:-1] + (tot_parts,),
        specs=[HBM] * 8 + [VMEM],
        outs=(HBM, VMEM),
        scratch=[
            vm((chip, width), BF16), blocks(crops, width), vm((EARLY, crops, width), BF16),
            vm((EARLY, chip, crops), BF16), vm((chip, width)),
            sems(1), sems(n_z), sems(EARLY), sems(EARLY),
        ],
        flops=2 * block_flops,
        limit=57,
    )
    parts = to_proto(msg)
    rmsg, gmsg = call(
        functools.partial(crops_kernel, n_z, n),
        (shape((n_z, 8, 128)), shape((n, size, width), BF16)),
        (parts, totals, p_sum, student_emb),
        scratch=[vm((8, 128)), vm((128, 128))],
    )
    rmsg, g_student, *late = tie((rmsg, g_student) + gathered)
    e_own, g_late = call(
        own_teacher_kernel,
        (shape((n_z - EARLY, chip, crops), BF16), shape((chip, width))),
        (prototypes,) + tuple(late)[EARLY:] + (tot_parts,),
        specs=[HBM] * (9 - EARLY) + [VMEM],
        outs=(HBM, VMEM),
        scratch=[
            vm((chip, width), BF16), vm((n_z - EARLY, crops, width), BF16),
            vm((crops, width), BF16), vm((n_z - EARLY, chip, crops), BF16),
            sems(1), sems(n_z - EARLY), sems(1), sems(n_z - EARLY),
        ],
        flops=block_flops,
        limit=57,
    )
    parts = to_z(rmsg)
    parts, gmsg, e_own = tie((parts, gmsg, e_own))
    pieces = to_proto(gmsg)
    keep, give = call(
        protos_kernel,
        (shape((owned + 8, width)),) * 2,
        (parts, e_early, e_own, g_student, g_late, col_parts, prototypes) + tuple(late),
        specs=[VMEM, HBM, HBM, VMEM, VMEM, VMEM, HBM] + [HBM] * 8,
        scratch=[
            vm((chip, width), BF16), vm((32, 128)), blocks(chip, crops), blocks(crops, width), vm((chip, width)),
            sems(1), sems(n_z), sems(n_z),
        ],
        flops=block_flops,
        limit=57,
    )
    got = swap(give)
    grad_protos = keep[:owned] + got[:owned]
    loss = (keep[owned:, :1] + got[owned:, :1]) * (-1.0 / (crops * n_dp))
    grad_student = pieces.astype(F32).reshape(crops, width)
    return grad_student, grad_protos[None], loss[0, 0]


def solution(mesh):
    fine = Mesh(np.asarray(mesh.devices).reshape(8, 2, 4, 4), ("z", "core", "y", "x"))
    in_specs = (P(CROPS, None), P(CROPS, None), P(PROTOS, None))
    out_specs = (P(CROPS, None), P(PROTOS, CROPS, None), P())
    return jax.shard_map(
        per_device, mesh=fine, in_specs=in_specs, out_specs=out_specs, check_vma=False
    )
```
